128 devices in a mesh: enc: 2 (over y_lo), ctx: 8 (over z, y_hi), tp: 8 (over x, core).
Axes of the slice: x: 4, y: 4 (y_hi: 2, y_lo: 2; y = y_hi * 2 + y_lo), z: 4, core: 2. Of those that a mesh axis runs over, the one named last changes fastest.
Arguments:
- query_rows: bfloat16 [12288, 6144], P(('enc', 'ctx', 'tp')), may hold values from -5 to 5
- key_rows: bfloat16 [12288, 6144], P(('enc', 'ctx', 'tp')), may hold values from -5 to 5
- value_rows: bfloat16 [12288, 6144], P(('enc', 'ctx', 'tp')), may hold values from -6 to 6
- out_grad: bfloat16 [12288, 6144], P(('enc', 'ctx', 'tp')), may hold values from -6 to 6
- clip_lengths: int32 [32], replicated, may hold values from 1 to 768, 12288 in all
Outputs:
- attended: bfloat16 [12288, 6144], P(('enc', 'ctx', 'tp'))
- query_grad: bfloat16 [12288, 6144], P(('enc', 'ctx', 'tp'))
- key_grad: bfloat16 [12288, 6144], P(('enc', 'ctx', 'tp'))
- value_grad: bfloat16 [12288, 6144], P(('enc', 'ctx', 'tp'))
The draws below stay inside these ranges and needn't reach their ends.
Inputs may be any that keep to these rules, and one draw needn't show every extreme that they name: `clip_lengths`: clip lengths sum to 12288; the longest clip has exactly 768 tokens.
All inputs are finite; a program needn't handle non-finite values.
Results may differ from the reference program's by a relative error of at most 0.011.
Values may be sent and summed in bfloat16 or wider, within the bound.
No kernel may reach another device: no remote copies, remote signals or barrier semaphores. Data moves between devices by JAX's collectives and lax.ppermute only.
A program may use at most 128 MiB of HBM per device.

```python
import math
import jax
import jax.numpy as jnp
import numpy as np
from jax import lax

DH = 128
ROWS = 768
F = 6144
LEN = 12288
CLIPS = 32


def draw_query_rows(key, part):
    drawn = jax.random.normal(jax.random.fold_in(key, 1), (LEN, F), jnp.float32)
    return jnp.clip(drawn, -5.0, 5.0).astype(jnp.bfloat16)


def draw_key_rows(key, part):
    drawn = jax.random.normal(jax.random.fold_in(key, 3), (LEN, F), jnp.float32)
    return jnp.clip(drawn, -5.0, 5.0).astype(jnp.bfloat16)


def level_of(key, extent, pieces, smallest, largest):
    def one(dim, parts):
        draws = jax.random.uniform(jax.random.fold_in(jax.random.fold_in(key, 6), dim), (parts,), jnp.float32, smallest / len(pieces), largest / len(pieces))
        return jnp.repeat(jnp.exp(draws), extent[dim] // parts).reshape((-1,) + (1,) * (len(extent) - dim - 1))

    factor_of = one(*pieces[0])
    for cut in pieces[1:]:
        factor_of = factor_of * one(*cut)
    return factor_of


def split_up(number_of, total, limit, skew):
    loads = [(1 << 20) // math.isqrt(grade ** skew) + 1 for grade in range(2, number_of + 1)]
    surplus, counts = total - limit - (number_of - 1), [1] * (number_of - 1)
    while surplus > 0:
        free = [i for i in range(number_of - 1) if counts[i] < limit]
        whole, remaining = sum([loads[i] for i in free]), surplus
        for i in free:
            more = min(limit - counts[i], max(1, remaining * loads[i] // whole), surplus)
            counts[i] = counts[i] + more
            surplus = surplus - more
    return np.array([limit] + counts)


def uneven_parts(rng, count, total, bound, lean):
    if count == 2:
        one = jax.random.randint(rng, (), max(1, total - bound), min(bound, total - 1) + 1)
        return jnp.stack([one, total - one])
    sizes = jnp.asarray(split_up(count, total, bound, lean), jnp.int32)
    twos = (count - 1) // 2
    source_of, receiver = sizes[1:1 + 2 * twos:2], sizes[2:2 + 2 * twos:2]
    slack = jnp.minimum(source_of - 1, bound - receiver)
    passed = jax.random.randint(jax.random.fold_in(rng, 1), (twos,), 0, 1 << 20) % (slack + 1)
    sizes = sizes.at[1:1 + 2 * twos:2].set(source_of - passed).at[2:2 + 2 * twos:2].set(receiver + passed)
    return sizes[jax.random.permutation(jax.random.fold_in(rng, 2), count)]


def normal_values(stream_key, dims, scale, limit, shards=(), kind=jnp.bfloat16):
    factor_of = level_of(stream_key, dims, shards, -0.22, 0.18) if shards else 1.0
    values = jax.random.normal(stream_key, dims, jnp.float32) * scale * factor_of
    return jnp.minimum(jnp.maximum(values, -limit), limit).astype(kind)


def setup_inputs(seed: int = 0) -> dict:
    key_of = jax.random.split(jax.random.key(seed), 6)
    return {
        "query_rows": draw_query_rows(jax.random.fold_in(key_of[5], 71), 0),
        "key_rows": draw_key_rows(jax.random.fold_in(key_of[5], 71), 0),
        "value_rows": normal_values(key_of[2], (LEN, F), 1.0, 6.0, ((0, 128),)),
        "out_grad": normal_values(key_of[3], (LEN, F), 1.0, 6.0, ((0, 128),)),
        "clip_lengths": uneven_parts(key_of[4], CLIPS, LEN, ROWS, 2).astype(jnp.int32),
    }


masked_score = -1.0e30


def clip_numbers(positions, clip_lengths):
    clip_ends = jnp.cumsum(clip_lengths).astype(jnp.int32)
    return jnp.sum((positions[:, None] >= clip_ends[None, :]).astype(jnp.int32), axis=1).astype(jnp.int32)


def window_pass(query_block, grad_block, key_window, value_window, allowed, score_scale):
    query_float = query_block.astype(jnp.float32)
    grad_float = grad_block.astype(jnp.float32)
    key_float = key_window.astype(jnp.float32)
    value_float = value_window.astype(jnp.float32)
    scores = jnp.einsum("ihd,jhd->hij", query_float, key_float) * score_scale
    scores = jnp.where(allowed[None], scores, masked_score)
    top_score = jnp.max(scores, axis=2, keepdims=True)
    log_total = top_score + jnp.log(jnp.sum(jnp.exp(scores - top_score), axis=2, keepdims=True))
    prob_float = jnp.where(allowed[None], jnp.exp(scores - log_total), 0.0)
    prob_half = lax.optimization_barrier(prob_float.astype(jnp.bfloat16)).astype(jnp.float32)
    out_float = jnp.einsum("hij,jhd->ihd", prob_half, value_float)
    correction = jnp.einsum("ihd,ihd->hi", grad_float, out_float)
    grad_prob = jnp.einsum("ihd,jhd->hij", grad_float, value_float)
    grad_score = (prob_float * (grad_prob - correction[:, :, None]) * score_scale).astype(jnp.bfloat16)
    grad_score = lax.optimization_barrier(grad_score).astype(jnp.float32)
    query_part = jnp.einsum("hij,jhd->ihd", grad_score, key_float).astype(jnp.bfloat16)
    key_part = jnp.einsum("hij,ihd->jhd", grad_score, query_float)
    value_part = jnp.einsum("hij,ihd->jhd", prob_half, grad_float)
    return out_float.astype(jnp.bfloat16), query_part, key_part, value_part


def reference(query_rows, key_rows, value_rows, out_grad, clip_lengths):
    head_count = F // DH
    head_shape = (LEN, head_count, DH)
    query_heads = query_rows.reshape(head_shape)
    grad_heads = out_grad.reshape(head_shape)
    padding = ((ROWS, ROWS), (0, 0), (0, 0))
    key_padded = jnp.pad(key_rows.reshape(head_shape), padding)
    value_padded = jnp.pad(value_rows.reshape(head_shape), padding)
    positions = jnp.arange(LEN + 2 * ROWS, dtype=jnp.int32) - ROWS
    clip_ids = clip_numbers(positions, clip_lengths)
    inside = (positions >= 0) & (positions < LEN)
    score_scale = DH ** -0.5

    def advance(carried, block_index):
        key_sum, value_sum = carried
        offset = (block_index * ROWS).astype(jnp.int32)
        query_block = lax.dynamic_slice_in_dim(query_heads, offset, ROWS, 0)
        grad_block = lax.dynamic_slice_in_dim(grad_heads, offset, ROWS, 0)
        key_window = lax.dynamic_slice_in_dim(key_padded, offset, 3 * ROWS, 0)
        value_window = lax.dynamic_slice_in_dim(value_padded, offset, 3 * ROWS, 0)
        window_ids = lax.dynamic_slice_in_dim(clip_ids, offset, 3 * ROWS, 0)
        window_inside = lax.dynamic_slice_in_dim(inside, offset, 3 * ROWS, 0)
        block_ids = lax.dynamic_slice_in_dim(clip_ids, offset + ROWS, ROWS, 0)
        allowed = (block_ids[:, None] == window_ids[None, :]) & window_inside[None, :]
        out_part, query_part, key_part, value_part = window_pass(query_block, grad_block, key_window, value_window, allowed, score_scale)
        key_sum = lax.dynamic_update_slice_in_dim(key_sum, lax.dynamic_slice_in_dim(key_sum, offset, 3 * ROWS, 0) + key_part, offset, 0)
        value_sum = lax.dynamic_update_slice_in_dim(value_sum, lax.dynamic_slice_in_dim(value_sum, offset, 3 * ROWS, 0) + value_part, offset, 0)
        return (key_sum, value_sum), (out_part, query_part)

    zeros = jnp.zeros((LEN + 2 * ROWS, head_count, DH), jnp.float32)
    (key_sum, value_sum), (outputs, query_parts) = lax.scan(advance, (zeros, zeros), jnp.arange(LEN // ROWS, dtype=jnp.int32))
    attended = outputs.reshape(LEN, F)
    query_grad = query_parts.reshape(LEN, F)
    key_grad = key_sum[ROWS:ROWS + LEN].astype(jnp.bfloat16).reshape(LEN, F)
    value_grad = value_sum[ROWS:ROWS + LEN].astype(jnp.bfloat16).reshape(LEN, F)
    return (attended, query_grad, key_grad, value_grad)
```

```python
import functools

import jax
import jax.numpy as jnp
from jax import lax
from jax.experimental import pallas as pl
from jax.experimental.pallas import tpu as pltpu
from jax.sharding import Mesh, PartitionSpec as P

DH = 128
ARRAYS = 4
TILE = 256
GROUP = ("yh", "tp")
CHAIN = ("yl", "z")
LONGEST = 768
LOG2E = 1.4426950408889634
MASKED = -1e30


def pack_kernel(q_ref, k_ref, v_ref, g_ref, o_ref):
    for j in range(o_ref.shape[0]):
        for a, ref in enumerate((q_ref, k_ref, v_ref, g_ref)):
            o_ref[j, a] = ref[:, j * DH : (j + 1) * DH]


def pack(chunk, members, arrays):
    rows = arrays[0].shape[0]
    step = 4
    steps = members // step
    spec = pl.BlockSpec((rows, step * DH), lambda i: (0, chunk * steps + i))
    size = members * ARRAYS * rows * DH
    return pl.pallas_call(
        pack_kernel,
        grid=(steps,),
        in_specs=[spec] * ARRAYS,
        out_specs=pl.BlockSpec((step, ARRAYS, rows, DH), lambda i: (i, 0, 0, 0)),
        out_shape=jax.ShapeDtypeStruct((members, ARRAYS, rows, DH), jnp.bfloat16),
        cost_estimate=pl.CostEstimate(flops=0, bytes_accessed=4 * size, transcendentals=0),
        name=f"pack{chunk}",
    )(*arrays)


def unpack_kernel(r_ref, *refs):
    outs = refs[-ARRAYS:]
    for j in range(r_ref.shape[0]):
        for a, ref in enumerate(outs):
            ref[:, j * DH : (j + 1) * DH] = r_ref[j, a]


def unpack(chunk, chunks, received, earlier):
    members, _, rows, _ = received.shape
    step = 4
    steps = members // step
    size = members * ARRAYS * rows * DH
    spec = pl.BlockSpec((rows, step * DH), lambda i: (0, chunk * steps + i))
    return pl.pallas_call(
        unpack_kernel,
        grid=(steps,),
        in_specs=[pl.BlockSpec((step, ARRAYS, rows, DH), lambda i: (i, 0, 0, 0))]
        + [pl.BlockSpec(memory_space=pl.ANY)] * len(earlier),
        out_specs=[spec] * ARRAYS,
        out_shape=[jax.ShapeDtypeStruct((rows, chunks * members * DH), jnp.bfloat16)] * ARRAYS,
        input_output_aliases={1 + a: a for a in range(len(earlier))},
        cost_estimate=pl.CostEstimate(flops=0, bytes_accessed=4 * size, transcendentals=0),
        name=f"unpack{chunk}",
    )(received, *earlier)


def attend_kernel(
    lo_ref,
    hi_ref,
    qid_ref,
    kid_ref,
    own_ref,
    before_ref,
    after_ref,
    result_ref,
    to_before_ref,
    to_after_ref,
    window,
    made,
    key_t,
    value_t,
    cells,
    key_sum,
    value_sum,
    in_sems,
    out_sems,
):
    edge = before_ref.shape[0]
    members, _, part, _ = own_ref.shape
    blocks = members + 2 * edge
    length = blocks * part
    tiles = length // TILE
    scale = DH**-0.5
    places = ((0, edge), (edge, members), (edge + members, edge))
    copies = [
        pltpu.make_async_copy(
            source.at[:, a], window.at[a, pl.ds(first, count)], in_sems.at[3 * a + n]
        )
        for a in range(ARRAYS)
        for n, (source, (first, count)) in enumerate(
            zip((before_ref, own_ref, after_ref), places)
        )
    ]
    for copy in copies:
        copy.start()
    key_sum[...] = jnp.zeros_like(key_sum)
    value_sum[...] = jnp.zeros_like(value_sum)
    for copy in copies:
        copy.wait()
    rows = window.reshape(ARRAYS, length, DH)
    outs = made.reshape(ARRAYS, length, DH)

    def turn(j, carry):
        at = pl.ds(pl.multiple_of(j * TILE, TILE), TILE)
        key_t[j] = rows[1, at, :].T
        value_t[j] = rows[2, at, :].T
        return carry

    lax.fori_loop(0, tiles, turn, 0)

    def nt(a, b):
        return lax.dot_general(a, b, (((1,), (1,)), ((), ())), preferred_element_type=jnp.float32)

    def nn(a, b):
        return jnp.dot(a, b, preferred_element_type=jnp.float32)

    def query_tile(t, carry):
        at = pl.ds(pl.multiple_of(t * TILE, TILE), TILE)
        low, high = lo_ref[t], hi_ref[t]

        @pl.when(low < high)
        def _():
            query, grad = rows[0, at, :], rows[3, at, :]
            query_ids = qid_ref[pl.ds(t, 1), :]

            def scores(j, top):
                keys = pl.ds(pl.multiple_of(j * TILE, TILE), TILE)
                dots = nt(rows[1, keys, :], query)
                ids = kid_ref[keys, :]
                ids = jnp.concatenate([ids] * (TILE // DH), axis=1)
                dots = jnp.where(ids == query_ids, dots, MASKED)
                cells[keys, :] = dots
                return jnp.maximum(top, jnp.max(dots, axis=0, keepdims=True))

            top = lax.fori_loop(low, high, scores, jnp.full((1, TILE), MASKED, jnp.float32))

            def weigh(j, sums):
                total, out_t = sums
                keys = pl.ds(pl.multiple_of(j * TILE, TILE), TILE)
                weights = jnp.exp2((cells[keys, :] - top) * (scale * LOG2E))
                cells[keys, :] = weights
                total = total + jnp.sum(weights, axis=0, keepdims=True)
                return total, out_t + nn(value_t[j], weights.astype(jnp.bfloat16))

            total, out_t = lax.fori_loop(
                low,
                high,
                weigh,
                (jnp.zeros((1, TILE), jnp.float32), jnp.zeros((DH, TILE), jnp.float32)),
            )
            inverse = jnp.where(query_ids >= 0, 1.0 / total, 0.0)
            out_t = out_t * inverse
            out = out_t.T
            correction = jnp.sum(grad.astype(jnp.float32).T * out_t, axis=0, keepdims=True)
            outs[0, at, :] = out.astype(jnp.bfloat16)
            scaled = inverse * scale

            def backward(j, query_grad_t):
                keys = pl.ds(pl.multiple_of(j * TILE, TILE), TILE)
                weights = cells[keys, :]
                prob = (weights * inverse).astype(jnp.bfloat16)
                value_sum[keys, :] += nn(prob, grad)
                grad_prob = nt(rows[2, keys, :], grad)
                grad_score = (weights * scaled * (grad_prob - correction)).astype(jnp.bfloat16)
                key_sum[keys, :] += nn(grad_score, query)
                return query_grad_t + nn(key_t[j], grad_score)

            query_grad_t = lax.fori_loop(
                low, high, backward, jnp.zeros((DH, TILE), jnp.float32)
            )
            outs[1, at, :] = query_grad_t.T.astype(jnp.bfloat16)

        return carry

    lax.fori_loop(0, tiles, query_tile, 0)

    def finish(j, carry):
        at = pl.ds(pl.multiple_of(j * TILE, TILE), TILE)
        outs[2, at, :] = key_sum[at, :].astype(jnp.bfloat16)
        outs[3, at, :] = value_sum[at, :].astype(jnp.bfloat16)
        return carry

    lax.fori_loop(0, tiles, finish, 0)
    copies = [
        pltpu.make_async_copy(
            made.at[a, pl.ds(first, count)], target.at[:, a], out_sems.at[3 * a + n]
        )
        for a in range(ARRAYS)
        for n, (target, (first, count)) in enumerate(
            zip((to_before_ref, result_ref, to_after_ref), places)
        )
    ]
    for copy in copies:
        copy.start()
    for copy in copies:
        copy.wait()


def attend(chunk, plan, own, before, after):
    low, high, query_ids, key_ids = plan
    members, _, part, _ = own.shape
    edge = before.shape[0]
    blocks = members + 2 * edge
    length = blocks * part
    tiles = length // TILE
    smem = pl.BlockSpec(memory_space=pltpu.SMEM)
    vmem = pl.BlockSpec(memory_space=pltpu.VMEM)
    hbm = pl.BlockSpec(memory_space=pl.ANY)
    pairs = tiles * 4 * TILE * TILE
    return pl.pallas_call(
        attend_kernel,
        in_specs=[smem, smem, vmem, vmem, hbm, hbm, hbm],
        out_specs=[hbm, hbm, hbm],
        out_shape=[
            jax.ShapeDtypeStruct(own.shape, jnp.bfloat16),
            jax.ShapeDtypeStruct(before.shape, jnp.bfloat16),
            jax.ShapeDtypeStruct(after.shape, jnp.bfloat16),
        ],
        scratch_shapes=[
            pltpu.VMEM((ARRAYS, blocks, part, DH), jnp.bfloat16),
            pltpu.VMEM((ARRAYS, blocks, part, DH), jnp.bfloat16),
            pltpu.VMEM((tiles, DH, TILE), jnp.bfloat16),
            pltpu.VMEM((tiles, DH, TILE), jnp.bfloat16),
            pltpu.VMEM((length, TILE), jnp.float32),
            pltpu.VMEM((length, DH), jnp.float32),
            pltpu.VMEM((length, DH), jnp.float32),
            pltpu.SemaphoreType.DMA((3 * ARRAYS,)),
            pltpu.SemaphoreType.DMA((3 * ARRAYS,)),
        ],
        compiler_params=pltpu.CompilerParams(vmem_limit_bytes=40 * 1024 * 1024),
        cost_estimate=pl.CostEstimate(
            flops=12 * pairs * DH, bytes_accessed=2 * ARRAYS * 2 * length * DH, transcendentals=pairs
        ),
        name=f"attend{chunk}",
    )(low, high, query_ids, key_ids, own, before, after)


def clip_plan(clip_lengths, shard, own_rows, edge_rows):
    count = clip_lengths.shape[0]
    order = jnp.arange(count, dtype=jnp.int32)
    upto = order[:, None] >= order[None, :]
    ends = jnp.sum(jnp.where(upto, clip_lengths[None, :], 0), axis=1)
    starts = ends - clip_lengths
    first, last = starts // own_rows, (ends - 1) // own_rows
    border = last * own_rows
    owner = jnp.where((first == last) | (ends - border > border - starts), last, first)
    mine = owner == shard
    length = own_rows + 2 * edge_rows
    origin = shard * own_rows - edge_rows
    positions = origin + jnp.arange(length, dtype=jnp.int32)
    inside = mine[None, :] & (positions[:, None] >= starts[None, :]) & (positions[:, None] < ends[None, :])
    ids = jnp.sum(jnp.where(inside, order[None, :] + 1, 0), axis=1) - 1
    tiles = length // TILE
    tile_from = origin + TILE * jnp.arange(tiles, dtype=jnp.int32)[:, None]
    meets = mine[None, :] & (starts[None, :] < tile_from + TILE) & (ends[None, :] > tile_from)
    low = jnp.min(jnp.where(meets, starts[None, :] - origin, length), axis=1) // TILE
    high = (jnp.max(jnp.where(meets, ends[None, :] - origin, 0), axis=1) + TILE - 1) // TILE
    query_ids = ids.reshape(tiles, TILE)
    key_ids = jnp.broadcast_to(ids[:, None], (length, DH))
    return (low, high, query_ids, key_ids), ids >= 0


def per_device(query_rows, key_rows, value_rows, out_grad, clip_lengths):
    part, features = query_rows.shape
    members = lax.axis_size(GROUP)
    chunks = features // (members * DH)
    shards = lax.axis_size(CHAIN)
    shard = lax.axis_index(CHAIN)
    own_rows = members * part
    edge = LONGEST // 2 // part
    plan, owned = clip_plan(clip_lengths, shard, own_rows, edge * part)
    owned = owned.reshape(members + 2 * edge, 1, part, 1)
    upward = [(i, i + 1) for i in range(shards - 1)]
    downward = [(i + 1, i) for i in range(shards - 1)]

    arrays = (query_rows, key_rows, value_rows, out_grad)
    results = ()
    arrived = [
        lax.all_to_all(pack(chunk, members, arrays), GROUP, 0, 0, tiled=True)
        for chunk in range(chunks)
    ]
    leaving = []
    for chunk, own in enumerate(arrived):
        before = lax.ppermute(own[members - edge :], CHAIN, upward)
        after = lax.ppermute(own[:edge], CHAIN, downward)
        made, to_before, to_after = attend(chunk, plan, own, before, after)
        head = lax.ppermute(to_after, CHAIN, upward)
        tail = lax.ppermute(to_before, CHAIN, downward)
        made = jnp.concatenate(
            [
                jnp.where(owned[edge : 2 * edge], made[:edge], head),
                made[edge : members - edge],
                jnp.where(owned[members : members + edge], made[members - edge :], tail),
            ]
        )
        leaving.append(lax.all_to_all(made, GROUP, 0, 0, tiled=True))
    for chunk, received in enumerate(leaving):
        results = unpack(chunk, chunks, received, results)
    return tuple(results)


def solution(mesh):
    enc, ctx, tp = mesh.devices.shape
    fine = Mesh(mesh.devices.reshape(enc, ctx // 2, 2, tp), ("yl", "z", "yh", "tp"))
    rows = P(("yl", "z", "yh", "tp"), None)
    return jax.shard_map(
        per_device,
        mesh=fine,
        in_specs=(rows,) * ARRAYS + (P(),),
        out_specs=(rows,) * ARRAYS,
        check_vma=False,
    )
```

```python
import functools

import jax
import jax.numpy as jnp
from jax import lax
from jax.experimental import pallas as pl
from jax.experimental.pallas import tpu as pltpu
from jax.sharding import Mesh, PartitionSpec as P

DH = 128
ARRAYS = 4
TILE = 256
GROUP = ("yh", "tp")
CHAIN = ("yl", "z")
LONGEST = 768
LOG2E = 1.4426950408889634
MASKED = -1e30


def pack_kernel(q_ref, k_ref, v_ref, g_ref, o_ref):
    for j in range(o_ref.shape[0]):
        for a, ref in enumerate((q_ref, k_ref, v_ref, g_ref)):
            o_ref[j, a] = ref[:, j * DH : (j + 1) * DH]


def pack(chunk, members, arrays):
    rows = arrays[0].shape[0]
    step = 4
    steps = members // step
    spec = pl.BlockSpec((rows, step * DH), lambda i: (0, chunk * steps + i))
    size = members * ARRAYS * rows * DH
    return pl.pallas_call(
        pack_kernel,
        grid=(steps,),
        in_specs=[spec] * ARRAYS,
        out_specs=pl.BlockSpec((step, ARRAYS, rows, DH), lambda i: (i, 0, 0, 0)),
        out_shape=jax.ShapeDtypeStruct((members, ARRAYS, rows, DH), jnp.bfloat16),
        cost_estimate=pl.CostEstimate(flops=0, bytes_accessed=4 * size, transcendentals=0),
        name=f"pack{chunk}",
    )(*arrays)


def unpack_kernel(r_ref, *refs):
    outs = refs[-ARRAYS:]
    for j in range(r_ref.shape[0]):
        for a, ref in enumerate(outs):
            ref[:, j * DH : (j + 1) * DH] = r_ref[j, a]


def unpack(chunk, chunks, received, earlier):
    members, _, rows, _ = received.shape
    step = 4
    steps = members // step
    size = members * ARRAYS * rows * DH
    spec = pl.BlockSpec((rows, step * DH), lambda i: (0, chunk * steps + i))
    return pl.pallas_call(
        unpack_kernel,
        grid=(steps,),
        in_specs=[pl.BlockSpec((step, ARRAYS, rows, DH), lambda i: (i, 0, 0, 0))]
        + [pl.BlockSpec(memory_space=pl.ANY)] * len(earlier),
        out_specs=[spec] * ARRAYS,
        out_shape=[jax.ShapeDtypeStruct((rows, chunks * members * DH), jnp.bfloat16)] * ARRAYS,
        input_output_aliases={1 + a: a for a in range(len(earlier))},
        cost_estimate=pl.CostEstimate(flops=0, bytes_accessed=4 * size, transcendentals=0),
        name=f"unpack{chunk}",
    )(received, *earlier)


def attend_kernel(
    lo_ref,
    hi_ref,
    qid_ref,
    kid_ref,
    own_ref,
    before_ref,
    after_ref,
    result_ref,
    to_before_ref,
    to_after_ref,
    window,
    made,
    key_t,
    value_t,
    cells,
    key_sum,
    value_sum,
    in_sems,
    out_sems,
):
    edge = before_ref.shape[0]
    members, _, part, _ = own_ref.shape
    blocks = members + 2 * edge
    length = blocks * part
    tiles = length // TILE
    scale = DH**-0.5
    places = ((0, edge), (edge, members), (edge + members, edge))
    copies = [
        pltpu.make_async_copy(
            source.at[:, a], window.at[a, pl.ds(first, count)], in_sems.at[3 * a + n]
        )
        for a in range(ARRAYS)
        for n, (source, (first, count)) in enumerate(
            zip((before_ref, own_ref, after_ref), places)
        )
    ]
    for copy in copies:
        copy.start()
    key_sum[...] = jnp.zeros_like(key_sum)
    value_sum[...] = jnp.zeros_like(value_sum)
    for copy in copies:
        copy.wait()
    rows = window.reshape(ARRAYS, length, DH)
    outs = made.reshape(ARRAYS, length, DH)

    def turn(j, carry):
        at = pl.ds(pl.multiple_of(j * TILE, TILE), TILE)
        key_t[j] = rows[1, at, :].T
        value_t[j] = rows[2, at, :].T
        return carry

    lax.fori_loop(0, tiles, turn, 0)

    def nt(a, b):
        return lax.dot_general(a, b, (((1,), (1,)), ((), ())), preferred_element_type=jnp.float32)

    def nn(a, b):
        return jnp.dot(a, b, preferred_element_type=jnp.float32)

    def query_tile(t, carry):
        at = pl.ds(pl.multiple_of(t * TILE, TILE), TILE)
        low, high = lo_ref[t], hi_ref[t]

        @pl.when(low < high)
        def _():
            query, grad = rows[0, at, :], rows[3, at, :]
            query_ids = qid_ref[pl.ds(t, 1), :]

            def scores(j, top):
                keys = pl.ds(pl.multiple_of(j * TILE, TILE), TILE)
                dots = nt(rows[1, keys, :], query)
                ids = kid_ref[keys, :]
                ids = jnp.concatenate([ids] * (TILE // DH), axis=1)
                dots = jnp.where(ids == query_ids, dots, MASKED)
                cells[keys, :] = dots
                return jnp.maximum(top, jnp.max(dots, axis=0, keepdims=True))

            top = lax.fori_loop(low, high, scores, jnp.full((1, TILE), MASKED, jnp.float32))

            def weigh(j, sums):
                total, out_t = sums
                keys = pl.ds(pl.multiple_of(j * TILE, TILE), TILE)
                weights = jnp.exp2((cells[keys, :] - top) * (scale * LOG2E))
                cells[keys, :] = weights
                total = total + jnp.sum(weights, axis=0, keepdims=True)
                return total, out_t + nn(value_t[j], weights.astype(jnp.bfloat16))

            total, out_t = lax.fori_loop(
                low,
                high,
                weigh,
                (jnp.zeros((1, TILE), jnp.float32), jnp.zeros((DH, TILE), jnp.float32)),
            )
            inverse = jnp.where(query_ids >= 0, 1.0 / total, 0.0)
            out_t = out_t * inverse
            out = out_t.T
            correction = jnp.sum(grad.astype(jnp.float32).T * out_t, axis=0, keepdims=True)
            outs[0, at, :] = out.astype(jnp.bfloat16)
            scaled = inverse * scale

            def backward(j, query_grad_t):
                keys = pl.ds(pl.multiple_of(j * TILE, TILE), TILE)
                weights = cells[keys, :]
                prob = (weights * inverse).astype(jnp.bfloat16)
                value_sum[keys, :] += nn(prob, grad)
                grad_prob = nt(rows[2, keys, :], grad)
                grad_score = (weights * scaled * (grad_prob - correction)).astype(jnp.bfloat16)
                key_sum[keys, :] += nn(grad_score, query)
                return query_grad_t + nn(key_t[j], grad_score)

            query_grad_t = lax.fori_loop(
                low, high, backward, jnp.zeros((DH, TILE), jnp.float32)
            )
            outs[1, at, :] = query_grad_t.T.astype(jnp.bfloat16)

        return carry

    lax.fori_loop(0, tiles, query_tile, 0)

    def finish(j, carry):
        at = pl.ds(pl.multiple_of(j * TILE, TILE), TILE)
        outs[2, at, :] = key_sum[at, :].astype(jnp.bfloat16)
        outs[3, at, :] = value_sum[at, :].astype(jnp.bfloat16)
        return carry

    lax.fori_loop(0, tiles, finish, 0)
    copies = [
        pltpu.make_async_copy(
            made.at[a, pl.ds(first, count)], target.at[:, a], out_sems.at[3 * a + n]
        )
        for a in range(ARRAYS)
        for n, (target, (first, count)) in enumerate(
            zip((to_before_ref, result_ref, to_after_ref), places)
        )
    ]
    for copy in copies:
        copy.start()
    for copy in copies:
        copy.wait()


def attend(chunk, plan, own, before, after):
    low, high, query_ids, key_ids = plan
    members, _, part, _ = own.shape
    edge = before.shape[0]
    blocks = members + 2 * edge
    length = blocks * part
    tiles = length // TILE
    smem = pl.BlockSpec(memory_space=pltpu.SMEM)
    vmem = pl.BlockSpec(memory_space=pltpu.VMEM)
    hbm = pl.BlockSpec(memory_space=pl.ANY)
    pairs = tiles * 4 * TILE * TILE
    return pl.pallas_call(
        attend_kernel,
        in_specs=[smem, smem, vmem, vmem, hbm, hbm, hbm],
        out_specs=[hbm, hbm, hbm],
        out_shape=[
            jax.ShapeDtypeStruct(own.shape, jnp.bfloat16),
            jax.ShapeDtypeStruct(before.shape, jnp.bfloat16),
            jax.ShapeDtypeStruct(after.shape, jnp.bfloat16),
        ],
        scratch_shapes=[
            pltpu.VMEM((ARRAYS, blocks, part, DH), jnp.bfloat16),
            pltpu.VMEM((ARRAYS, blocks, part, DH), jnp.bfloat16),
            pltpu.VMEM((tiles, DH, TILE), jnp.bfloat16),
            pltpu.VMEM((tiles, DH, TILE), jnp.bfloat16),
            pltpu.VMEM((length, TILE), jnp.float32),
            pltpu.VMEM((length, DH), jnp.float32),
            pltpu.VMEM((length, DH), jnp.float32),
            pltpu.SemaphoreType.DMA((3 * ARRAYS,)),
            pltpu.SemaphoreType.DMA((3 * ARRAYS,)),
        ],
        compiler_params=pltpu.CompilerParams(vmem_limit_bytes=40 * 1024 * 1024),
        cost_estimate=pl.CostEstimate(
            flops=12 * pairs * DH, bytes_accessed=2 * ARRAYS * 2 * length * DH, transcendentals=pairs
        ),
        name=f"attend{chunk}",
    )(low, high, query_ids, key_ids, own, before, after)


def merge_kernel(kid_ref, made_ref, head_ref, tail_ref, o_ref):
    at_head = pl.program_id(0) == 0
    for j in range(o_ref.shape[0]):
        mine = kid_ref[j] >= 0
        for a in range(ARRAYS):
            here = made_ref[j, a].astype(jnp.float32)
            came = jnp.where(
                at_head, head_ref[j, a].astype(jnp.float32), tail_ref[j, a].astype(jnp.float32)
            )
            o_ref[j, a] = jnp.where(mine, here, came).astype(jnp.bfloat16)


def merge(chunk, plan, made, head, tail):
    members, _, part, _ = made.shape
    edge = head.shape[0]
    far = members // edge - 1
    block = (edge, ARRAYS, part, DH)
    key_ids = plan[-1].reshape(-1, part, DH)
    spec = pl.BlockSpec(block, lambda i: (far * i, 0, 0, 0))
    whole = pl.BlockSpec(block, lambda i: (0, 0, 0, 0))
    return pl.pallas_call(
        merge_kernel,
        grid=(2,),
        in_specs=[pl.BlockSpec((edge, part, DH), lambda i: (1 + far * i, 0, 0)), spec, whole, whole],
        out_specs=spec,
        out_shape=jax.ShapeDtypeStruct(made.shape, jnp.bfloat16),
        input_output_aliases={1: 0},
        cost_estimate=pl.CostEstimate(
            flops=0, bytes_accessed=12 * edge * ARRAYS * part * DH, transcendentals=0
        ),
        name=f"merge{chunk}",
    )(key_ids, made, head, tail)


def clip_plan(clip_lengths, shard, own_rows, edge_rows):
    count = clip_lengths.shape[0]
    order = jnp.arange(count, dtype=jnp.int32)
    upto = order[:, None] >= order[None, :]
    ends = jnp.sum(jnp.where(upto, clip_lengths[None, :], 0), axis=1)
    starts = ends - clip_lengths
    first, last = starts // own_rows, (ends - 1) // own_rows
    border = last * own_rows
    owner = jnp.where((first == last) | (ends - border > border - starts), last, first)
    mine = owner == shard
    length = own_rows + 2 * edge_rows
    origin = shard * own_rows - edge_rows
    positions = origin + jnp.arange(length, dtype=jnp.int32)
    inside = mine[None, :] & (positions[:, None] >= starts[None, :]) & (positions[:, None] < ends[None, :])
    ids = jnp.sum(jnp.where(inside, order[None, :] + 1, 0), axis=1) - 1
    tiles = length // TILE
    tile_from = origin + TILE * jnp.arange(tiles, dtype=jnp.int32)[:, None]
    meets = mine[None, :] & (starts[None, :] < tile_from + TILE) & (ends[None, :] > tile_from)
    low = jnp.min(jnp.where(meets, starts[None, :] - origin, length), axis=1) // TILE
    high = (jnp.max(jnp.where(meets, ends[None, :] - origin, 0), axis=1) + TILE - 1) // TILE
    query_ids = ids.reshape(tiles, TILE)
    key_ids = jnp.broadcast_to(ids[:, None], (length, DH))
    return (low, high, query_ids, key_ids), ids >= 0


def per_device(query_rows, key_rows, value_rows, out_grad, clip_lengths):
    part, features = query_rows.shape
    members = lax.axis_size(GROUP)
    chunks = features // (members * DH)
    shards = lax.axis_size(CHAIN)
    shard = lax.axis_index(CHAIN)
    own_rows = members * part
    edge = LONGEST // 2 // part
    plan, owned = clip_plan(clip_lengths, shard, own_rows, edge * part)
    owned = owned.reshape(members + 2 * edge, 1, part, 1)
    upward = [(i, i + 1) for i in range(shards - 1)]
    downward = [(i + 1, i) for i in range(shards - 1)]

    arrays = (query_rows, key_rows, value_rows, out_grad)
    tie = lax.optimization_barrier
    swap = functools.partial(lax.all_to_all, axis_name=GROUP, split_axis=0, concat_axis=0, tiled=True)

    def compute(chunk, own):
        before = lax.ppermute(own[members - edge :], CHAIN, upward)
        after = lax.ppermute(own[:edge], CHAIN, downward)
        return attend(chunk, plan, own, before, after)

    def settle(chunk, parts):
        made, to_before, to_after = parts
        head = lax.ppermute(to_after, CHAIN, upward)
        tail = lax.ppermute(to_before, CHAIN, downward)
        return merge(chunk, plan, made, head, tail)

    packed = [pack(chunk, members, arrays) for chunk in range(chunks)]
    own, made, ready, got = {}, {}, {}, {}
    own[0] = swap(packed[0])
    for chunk in range(1, chunks):
        if chunk >= 2:
            packed[chunk], own[chunk - 1], made[chunk - 2] = tie(
                (packed[chunk], own[chunk - 1], made[chunk - 2])
            )
            ready[chunk - 2] = settle(chunk - 2, made[chunk - 2])
        else:
            packed[chunk], own[chunk - 1] = tie((packed[chunk], own[chunk - 1]))
        own[chunk] = swap(packed[chunk])
        made[chunk - 1] = compute(chunk - 1, own[chunk - 1])
    last = chunks - 1
    results = ()
    for chunk in range(chunks):
        if chunk == 0:
            ready[0], own[last], made[last - 1] = tie((ready[0], own[last], made[last - 1]))
            ready[last - 1] = settle(last - 1, made[last - 1])
            made[last] = compute(last, own[last])
        elif chunk == 1:
            ready[1], got[0], made[last] = tie((ready[1], got[0], made[last]))
            ready[last] = settle(last, made[last])
        else:
            ready[chunk], got[chunk - 1] = tie((ready[chunk], got[chunk - 1]))
        got[chunk] = swap(ready[chunk])
        if chunk:
            results = unpack(chunk - 1, chunks, got[chunk - 1], results)
    return tuple(unpack(last, chunks, got[last], results))


def solution(mesh):
    enc, ctx, tp = mesh.devices.shape
    fine = Mesh(mesh.devices.reshape(enc, ctx // 2, 2, tp), ("yl", "z", "yh", "tp"))
    rows = P(("yl", "z", "yh", "tp"), None)
    return jax.shard_map(
        per_device,
        mesh=fine,
        in_specs=(rows,) * ARRAYS + (P(),),
        out_specs=(rows,) * ARRAYS,
        check_vma=False,
    )
```

```python
import functools

import jax
import jax.numpy as jnp
from jax import lax
from jax.experimental import pallas as pl
from jax.experimental.pallas import tpu as pltpu
from jax.sharding import Mesh, PartitionSpec as P

DH = 128
ARRAYS = 4
TILE = 256
WIDTHS = (2, 3, 4, 5, 6, 8)
GROUP = ("yh", "tp")
CHAIN = ("yl", "z")
LONGEST = 768
LOG2E = 1.4426950408889634
MASKED = -1e30


def pack_kernel(q_ref, k_ref, v_ref, g_ref, o_ref):
    for j in range(o_ref.shape[0]):
        for a, ref in enumerate((q_ref, k_ref, v_ref, g_ref)):
            o_ref[j, a] = ref[:, j * DH : (j + 1) * DH]


def pack(chunk, members, arrays):
    rows = arrays[0].shape[0]
    step = 4
    steps = members // step
    spec = pl.BlockSpec((rows, step * DH), lambda i: (0, chunk * steps + i))
    size = members * ARRAYS * rows * DH
    return pl.pallas_call(
        pack_kernel,
        grid=(steps,),
        in_specs=[spec] * ARRAYS,
        out_specs=pl.BlockSpec((step, ARRAYS, rows, DH), lambda i: (i, 0, 0, 0)),
        out_shape=jax.ShapeDtypeStruct((members, ARRAYS, rows, DH), jnp.bfloat16),
        cost_estimate=pl.CostEstimate(flops=0, bytes_accessed=4 * size, transcendentals=0),
        name=f"pack{chunk}",
    )(*arrays)


def unpack_kernel(r_ref, *refs):
    outs = refs[-ARRAYS:]
    for j in range(r_ref.shape[0]):
        for a, ref in enumerate(outs):
            ref[:, j * DH : (j + 1) * DH] = r_ref[j, a]


def unpack(chunk, chunks, received, earlier):
    members, _, rows, _ = received.shape
    step = 4
    steps = members // step
    size = members * ARRAYS * rows * DH
    spec = pl.BlockSpec((rows, step * DH), lambda i: (0, chunk * steps + i))
    return pl.pallas_call(
        unpack_kernel,
        grid=(steps,),
        in_specs=[pl.BlockSpec((step, ARRAYS, rows, DH), lambda i: (i, 0, 0, 0))]
        + [pl.BlockSpec(memory_space=pl.ANY)] * len(earlier),
        out_specs=[spec] * ARRAYS,
        out_shape=[jax.ShapeDtypeStruct((rows, chunks * members * DH), jnp.bfloat16)] * ARRAYS,
        input_output_aliases={1 + a: a for a in range(len(earlier))},
        cost_estimate=pl.CostEstimate(flops=0, bytes_accessed=4 * size, transcendentals=0),
        name=f"unpack{chunk}",
    )(received, *earlier)


def attend_kernel(
    lo_ref,
    hi_ref,
    qid_ref,
    kid_ref,
    own_ref,
    before_ref,
    after_ref,
    result_ref,
    to_before_ref,
    to_after_ref,
    window,
    made,
    key_t,
    value_t,
    cells,
    key_sum,
    value_sum,
    in_sems,
    out_sems,
):
    edge = before_ref.shape[0]
    members, _, part, _ = own_ref.shape
    blocks = members + 2 * edge
    length = blocks * part
    tiles = length // TILE
    scale = DH**-0.5
    places = ((0, edge), (edge, members), (edge + members, edge))
    copies = [
        pltpu.make_async_copy(
            source.at[:, a], window.at[a, pl.ds(first, count)], in_sems.at[3 * a + n]
        )
        for a in range(ARRAYS)
        for n, (source, (first, count)) in enumerate(
            zip((before_ref, own_ref, after_ref), places)
        )
    ]
    for copy in copies:
        copy.start()
    key_sum[...] = jnp.zeros_like(key_sum)
    value_sum[...] = jnp.zeros_like(value_sum)
    for copy in copies:
        copy.wait()
    rows = window.reshape(ARRAYS, length, DH)
    outs = made.reshape(ARRAYS, length, DH)

    def turn(j, carry):
        at = pl.ds(pl.multiple_of(j * TILE, TILE), TILE)
        key_t[:, at] = rows[1, at, :].T
        value_t[:, at] = rows[2, at, :].T
        return carry

    lax.fori_loop(0, tiles, turn, 0)

    def nt(a, b):
        return lax.dot_general(a, b, (((1,), (1,)), ((), ())), preferred_element_type=jnp.float32)

    def nn(a, b):
        return jnp.dot(a, b, preferred_element_type=jnp.float32)

    def query_tile(t, nothing):
        at = pl.ds(pl.multiple_of(t * TILE, TILE), TILE)
        low, count = lo_ref[t], hi_ref[t] - lo_ref[t]

        def tile_of(width):
            size = width * TILE
            first = jnp.minimum(low, tiles - width) * TILE
            keys = pl.ds(pl.multiple_of(first, TILE), size)
            query, grad = rows[0, at, :], rows[3, at, :]
            query_ids = qid_ref[pl.ds(t, 1), :]
            dots = nt(rows[1, keys, :], query)
            ids = kid_ref[keys, :]
            ids = jnp.concatenate([ids] * (TILE // DH), axis=1)
            dots = jnp.where(ids == query_ids, dots, MASKED)
            top = jnp.max(dots, axis=0, keepdims=True)
            weights = jnp.exp2((dots - top) * (scale * LOG2E))
            total = jnp.sum(weights, axis=0, keepdims=True)
            inverse = jnp.where(query_ids >= 0, 1.0 / total, 0.0)
            prob = weights * inverse
            half = prob.astype(jnp.bfloat16)
            out_t = nn(value_t[:, keys], half)
            grad_prob = nt(rows[2, keys, :], grad)
            correction = jnp.sum(grad.astype(jnp.float32).T * out_t, axis=0, keepdims=True)
            outs[0, at, :] = out_t.T.astype(jnp.bfloat16)
            value_sum[keys, :] += nn(half, grad)
            grad_dots = (prob * (grad_prob - correction)).astype(jnp.bfloat16)
            key_sum[keys, :] += nn(grad_dots, query)
            query_grad_t = nn(key_t[:, keys], grad_dots)
            outs[1, at, :] = (query_grad_t * scale).T.astype(jnp.bfloat16)

        smaller = 0
        for width in WIDTHS:
            pl.when((count > smaller) & (count <= width))(functools.partial(tile_of, width))
            smaller = width
        return nothing

    lax.fori_loop(0, tiles, query_tile, 0)

    def finish(j, carry):
        at = pl.ds(pl.multiple_of(j * TILE, TILE), TILE)
        outs[2, at, :] = (key_sum[at, :] * scale).astype(jnp.bfloat16)
        outs[3, at, :] = value_sum[at, :].astype(jnp.bfloat16)
        return carry

    lax.fori_loop(0, tiles, finish, 0)
    copies = [
        pltpu.make_async_copy(
            made.at[a, pl.ds(first, count)], target.at[:, a], out_sems.at[3 * a + n]
        )
        for a in range(ARRAYS)
        for n, (target, (first, count)) in enumerate(
            zip((to_before_ref, result_ref, to_after_ref), places)
        )
    ]
    for copy in copies:
        copy.start()
    for copy in copies:
        copy.wait()


def attend(chunk, plan, own, before, after):
    low, high, query_ids, key_ids = plan
    members, _, part, _ = own.shape
    edge = before.shape[0]
    blocks = members + 2 * edge
    length = blocks * part
    tiles = length // TILE
    smem = pl.BlockSpec(memory_space=pltpu.SMEM)
    vmem = pl.BlockSpec(memory_space=pltpu.VMEM)
    hbm = pl.BlockSpec(memory_space=pl.ANY)
    pairs = tiles * 4 * TILE * TILE
    return pl.pallas_call(
        attend_kernel,
        in_specs=[smem, smem, vmem, vmem, hbm, hbm, hbm],
        out_specs=[hbm, hbm, hbm],
        out_shape=[
            jax.ShapeDtypeStruct(own.shape, jnp.bfloat16),
            jax.ShapeDtypeStruct(before.shape, jnp.bfloat16),
            jax.ShapeDtypeStruct(after.shape, jnp.bfloat16),
        ],
        scratch_shapes=[
            pltpu.VMEM((ARRAYS, blocks, part, DH), jnp.bfloat16),
            pltpu.VMEM((ARRAYS, blocks, part, DH), jnp.bfloat16),
            pltpu.VMEM((DH, length), jnp.bfloat16),
            pltpu.VMEM((DH, length), jnp.bfloat16),
            pltpu.VMEM((length, TILE), jnp.float32),
            pltpu.VMEM((length, DH), jnp.float32),
            pltpu.VMEM((length, DH), jnp.float32),
            pltpu.SemaphoreType.DMA((3 * ARRAYS,)),
            pltpu.SemaphoreType.DMA((3 * ARRAYS,)),
        ],
        compiler_params=pltpu.CompilerParams(vmem_limit_bytes=40 * 1024 * 1024),
        cost_estimate=pl.CostEstimate(
            flops=12 * pairs * DH, bytes_accessed=2 * ARRAYS * 2 * length * DH, transcendentals=pairs
        ),
        name=f"attend{chunk}",
    )(low, high, query_ids, key_ids, own, before, after)


def merge_kernel(kid_ref, made_ref, head_ref, tail_ref, o_ref):
    at_head = pl.program_id(0) == 0
    for j in range(o_ref.shape[0]):
        part = o_ref.shape[2]
        mine = kid_ref[j * part : (j + 1) * part] >= 0
        for a in range(ARRAYS):
            here = made_ref[j, a].astype(jnp.float32)
            came = jnp.where(
                at_head, head_ref[j, a].astype(jnp.float32), tail_ref[j, a].astype(jnp.float32)
            )
            o_ref[j, a] = jnp.where(mine, here, came).astype(jnp.bfloat16)


def merge(chunk, plan, made, head, tail):
    members, _, part, _ = made.shape
    edge = head.shape[0]
    far = members // edge - 1
    block = (edge, ARRAYS, part, DH)
    key_ids = plan[-1]
    spec = pl.BlockSpec(block, lambda i: (far * i, 0, 0, 0))
    whole = pl.BlockSpec(block, lambda i: (0, 0, 0, 0))
    return pl.pallas_call(
        merge_kernel,
        grid=(2,),
        in_specs=[pl.BlockSpec((edge * part, DH), lambda i: (1 + far * i, 0)), spec, whole, whole],
        out_specs=spec,
        out_shape=jax.ShapeDtypeStruct(made.shape, jnp.bfloat16),
        input_output_aliases={1: 0},
        cost_estimate=pl.CostEstimate(
            flops=0, bytes_accessed=12 * edge * ARRAYS * part * DH, transcendentals=0
        ),
        name=f"merge{chunk}",
    )(key_ids, made, head, tail)


def clip_plan(clip_lengths, shard, own_rows, edge_rows):
    count = clip_lengths.shape[0]
    order = jnp.arange(count, dtype=jnp.int32)
    upto = order[:, None] >= order[None, :]
    ends = jnp.sum(jnp.where(upto, clip_lengths[None, :], 0), axis=1)
    starts = ends - clip_lengths
    first, last = starts // own_rows, (ends - 1) // own_rows
    border = last * own_rows
    owner = jnp.where((first == last) | (ends - border > border - starts), last, first)
    mine = owner == shard
    length = own_rows + 2 * edge_rows
    origin = shard * own_rows - edge_rows
    positions = origin + jnp.arange(length, dtype=jnp.int32)
    inside = mine[None, :] & (positions[:, None] >= starts[None, :]) & (positions[:, None] < ends[None, :])
    ids = jnp.sum(jnp.where(inside, order[None, :] + 1, 0), axis=1) - 1
    tiles = length // TILE
    tile_from = origin + TILE * jnp.arange(tiles, dtype=jnp.int32)[:, None]
    meets = mine[None, :] & (starts[None, :] < tile_from + TILE) & (ends[None, :] > tile_from)
    low = jnp.min(jnp.where(meets, starts[None, :] - origin, length), axis=1) // TILE
    high = (jnp.max(jnp.where(meets, ends[None, :] - origin, 0), axis=1) + TILE - 1) // TILE
    query_ids = ids.reshape(tiles, TILE)
    key_ids = jnp.broadcast_to(ids[:, None], (length, DH))
    return (low, high, query_ids, key_ids), ids >= 0


def per_device(query_rows, key_rows, value_rows, out_grad, clip_lengths):
    part, features = query_rows.shape
    members = lax.axis_size(GROUP)
    chunks = features // (members * DH)
    shards = lax.axis_size(CHAIN)
    shard = lax.axis_index(CHAIN)
    own_rows = members * part
    edge = LONGEST // 2 // part
    plan, owned = clip_plan(clip_lengths, shard, own_rows, edge * part)
    owned = owned.reshape(members + 2 * edge, 1, part, 1)
    upward = [(i, i + 1) for i in range(shards - 1)]
    downward = [(i + 1, i) for i in range(shards - 1)]

    arrays = (query_rows, key_rows, value_rows, out_grad)
    tie = lax.optimization_barrier
    swap = functools.partial(lax.all_to_all, axis_name=GROUP, split_axis=0, concat_axis=0, tiled=True)

    def around(own):
        return (
            lax.ppermute(own[members - edge :], CHAIN, upward),
            lax.ppermute(own[:edge], CHAIN, downward),
        )

    def back(parts):
        made, to_before, to_after = parts
        head = lax.ppermute(to_after, CHAIN, upward)
        return made, head, lax.ppermute(to_before, CHAIN, downward)

    packed = [pack(chunk, members, arrays) for chunk in range(chunks)]
    last = chunks - 1
    own, halo, made, sent, ready, got = {}, {}, {}, {}, {}, {}
    for chunk in range(chunks):
        if chunk >= 2:
            packed[chunk], own[chunk - 1], halo[chunk - 2] = tie(
                (packed[chunk], own[chunk - 1], halo[chunk - 2])
            )
        elif chunk:
            packed[chunk], own[chunk - 1] = tie((packed[chunk], own[chunk - 1]))
        own[chunk] = swap(packed[chunk])
        if chunk:
            halo[chunk - 1] = around(own[chunk - 1])
    halo[last] = around(own[last])
    for chunk in range(chunks):
        inputs = (own[chunk], halo[chunk])
        if chunk == 0:
            inputs, own[1] = tie((inputs, own[1]))
        elif chunk < last:
            inputs, made[chunk - 1], own[chunk + 1] = tie((inputs, made[chunk - 1], own[chunk + 1]))
        else:
            inputs, ready[chunk - 2] = tie((inputs, ready[chunk - 2]))
            got[0] = swap(ready[0])
        made[chunk] = attend(chunk, plan, inputs[0], *inputs[1])
        if chunk:
            sent[chunk - 1], made[chunk] = tie((sent[chunk - 1], made[chunk]))
            ready[chunk - 1] = merge(chunk - 1, plan, *sent[chunk - 1])
        sent[chunk] = back(made[chunk])
    results = ()
    for chunk in range(1, chunks):
        if chunk == last:
            ready[last] = merge(last, plan, *sent[last])
        ready[chunk], got[chunk - 1] = tie((ready[chunk], got[chunk - 1]))
        got[chunk] = swap(ready[chunk])
        results = unpack(chunk - 1, chunks, got[chunk - 1], results)
    return tuple(unpack(last, chunks, got[last], results))


def solution(mesh):
    enc, ctx, tp = mesh.devices.shape
    fine = Mesh(mesh.devices.reshape(enc, ctx // 2, 2, tp), ("yl", "z", "yh", "tp"))
    rows = P(("yl", "z", "yh", "tp"), None)
    return jax.shard_map(
        per_device,
        mesh=fine,
        in_specs=(rows,) * ARRAYS + (P(),),
        out_specs=(rows,) * ARRAYS,
        check_vma=False,
    )
```

```python
import functools

import jax
import jax.numpy as jnp
from jax import lax
from jax.experimental import pallas as pl
from jax.experimental.pallas import tpu as pltpu
from jax.sharding import Mesh, PartitionSpec as P

DH = 128
ARRAYS = 4
TILE = 256
WIDTHS = {False: (2, 3, 4, 6), True: (2, 3, 4)}
GROUP = ("yh", "tp")
CHAIN = ("yl", "z")
LONGEST = 768
LOG2E = 1.4426950408889634
MASKED = -1e30


def pack_kernel(q_ref, k_ref, v_ref, g_ref, o_ref):
    for j in range(o_ref.shape[0]):
        for a, ref in enumerate((q_ref, k_ref, v_ref, g_ref)):
            o_ref[j, a] = ref[:, j * DH : (j + 1) * DH]


def pack(chunk, members, arrays):
    rows = arrays[0].shape[0]
    step = members
    steps = members // step
    spec = pl.BlockSpec((rows, step * DH), lambda i: (0, chunk * steps + i))
    size = members * ARRAYS * rows * DH
    return pl.pallas_call(
        pack_kernel,
        grid=(steps,),
        in_specs=[spec] * ARRAYS,
        out_specs=pl.BlockSpec((step, ARRAYS, rows, DH), lambda i: (i, 0, 0, 0)),
        out_shape=jax.ShapeDtypeStruct((members, ARRAYS, rows, DH), jnp.bfloat16),
        cost_estimate=pl.CostEstimate(flops=0, bytes_accessed=4 * size, transcendentals=0),
        name=f"pack{chunk}",
    )(*arrays)


def unpack_kernel(r_ref, *refs):
    outs = refs[-ARRAYS:]
    for j in range(r_ref.shape[0]):
        for a, ref in enumerate(outs):
            ref[:, j * DH : (j + 1) * DH] = r_ref[j, a]


def unpack(chunk, chunks, received, earlier):
    members, _, rows, _ = received.shape
    step = members
    steps = members // step
    size = members * ARRAYS * rows * DH
    spec = pl.BlockSpec((rows, step * DH), lambda i: (0, chunk * steps + i))
    return pl.pallas_call(
        unpack_kernel,
        grid=(steps,),
        in_specs=[pl.BlockSpec(memory_space=pltpu.VMEM)]
        + [pl.BlockSpec(memory_space=pl.ANY)] * len(earlier),
        out_specs=[spec] * ARRAYS,
        out_shape=[jax.ShapeDtypeStruct((rows, chunks * members * DH), jnp.bfloat16)] * ARRAYS,
        input_output_aliases={1 + a: a for a in range(len(earlier))},
        cost_estimate=pl.CostEstimate(flops=0, bytes_accessed=4 * size, transcendentals=0),
        name=f"unpack{chunk}",
    )(received, *earlier)


def attend_kernel(edge, *refs):
    lo_ref, hi_ref, qid_ref, kid_ref, own_ref = refs[:5]
    if edge:
        before_ref, after_ref, base_ref, result_ref, to_before_ref, to_after_ref = refs[5:11]
    else:
        result_ref = refs[5]
    window, made, key_t, value_t, key_sum, value_sum, cells = refs[-7:]
    members, _, part, _ = own_ref.shape
    blocks = members + 2 * edge
    length = blocks * part
    tiles = length // TILE
    scale = DH**-0.5
    pieces = [(own_ref, edge)]
    if edge:
        pieces += [(before_ref, 0), (after_ref, edge + members)]
        for i in range(members):
            for a in range(ARRAYS):
                made[a, edge + i] = base_ref[i, a]
    for source, first in pieces:
        for i in range(source.shape[0]):
            for a in range(ARRAYS):
                window[a, first + i] = source[i, a]
    key_sum[...] = jnp.zeros_like(key_sum)
    value_sum[...] = jnp.zeros_like(value_sum)
    rows = window.reshape(ARRAYS, length, DH)
    outs = made.reshape(ARRAYS, length, DH)

    def put(a, at, new):
        if edge:
            new = jnp.where(kid_ref[at, :] >= 0, new, outs[a, at, :].astype(jnp.float32))
        outs[a, at, :] = new.astype(jnp.bfloat16)

    def turn(j, carry):
        at = pl.ds(pl.multiple_of(j * TILE, TILE), TILE)
        key_t[:, at] = rows[1, at, :].T
        value_t[:, at] = rows[2, at, :].T
        return carry

    lax.fori_loop(0, tiles, turn, 0)

    def nt(a, b):
        return lax.dot_general(a, b, (((1,), (1,)), ((), ())), preferred_element_type=jnp.float32)

    def nn(a, b):
        return jnp.dot(a, b, preferred_element_type=jnp.float32)

    def query_tile(t, nothing):
        at = pl.ds(pl.multiple_of(t * TILE, TILE), TILE)
        low, count = lo_ref[t], hi_ref[t] - lo_ref[t]

        def tile_of(width):
            size = width * TILE
            first = jnp.minimum(low, tiles - width) * TILE
            keys = pl.ds(pl.multiple_of(first, TILE), size)
            query, grad = rows[0, at, :], rows[3, at, :]
            query_ids = qid_ref[pl.ds(t, 1), :]
            dots = nt(rows[1, keys, :], query)
            ids = kid_ref[keys, :]
            ids = jnp.concatenate([ids] * (TILE // DH), axis=1)
            dots = jnp.where(ids == query_ids, dots, MASKED)
            top = jnp.max(dots, axis=0, keepdims=True)
            weights = jnp.exp2((dots - top) * (scale * LOG2E))
            total = jnp.sum(weights, axis=0, keepdims=True)
            inverse = jnp.where(query_ids >= 0, 1.0 / total, 0.0)
            prob = weights * inverse
            half = prob.astype(jnp.bfloat16)
            out_t = nn(value_t[:, keys], half)
            grad_prob = nt(rows[2, keys, :], grad)
            correction = jnp.sum(grad.astype(jnp.float32).T * out_t, axis=0, keepdims=True)
            put(0, at, out_t.T)
            value_sum[keys, :] += nn(half, grad)
            grad_dots = (prob * (grad_prob - correction)).astype(jnp.bfloat16)
            key_sum[keys, :] += nn(grad_dots, query)
            query_grad_t = nn(key_t[:, keys], grad_dots)
            put(1, at, (query_grad_t * scale).T)

        def tile_by_steps():
            query, grad = rows[0, at, :], rows[3, at, :]
            query_ids = qid_ref[pl.ds(t, 1), :]

            def over_keys(body, carry):
                def step(j, carry):
                    return body(pl.ds(pl.multiple_of(j * TILE, TILE), TILE), carry)

                return lax.fori_loop(low, low + count, step, carry)

            def scores(keys, top):
                dots = nt(rows[1, keys, :], query)
                ids = kid_ref[keys, :]
                ids = jnp.concatenate([ids] * (TILE // DH), axis=1)
                dots = jnp.where(ids == query_ids, dots, MASKED)
                cells[keys, :] = dots
                return jnp.maximum(top, jnp.max(dots, axis=0, keepdims=True))

            top = over_keys(scores, jnp.full((1, TILE), MASKED, jnp.float32))

            def weigh(keys, sums):
                total, out_t = sums
                weights = jnp.exp2((cells[keys, :] - top) * (scale * LOG2E))
                cells[keys, :] = weights
                total = total + jnp.sum(weights, axis=0, keepdims=True)
                return total, out_t + nn(value_t[:, keys], weights.astype(jnp.bfloat16))

            zero = jnp.zeros((DH, TILE), jnp.float32)
            total, out_t = over_keys(weigh, (jnp.zeros((1, TILE), jnp.float32), zero))
            inverse = jnp.where(query_ids >= 0, 1.0 / total, 0.0)
            out_t = out_t * inverse
            correction = jnp.sum(grad.astype(jnp.float32).T * out_t, axis=0, keepdims=True)
            put(0, at, out_t.T)

            def backward(keys, query_grad_t):
                prob = cells[keys, :] * inverse
                value_sum[keys, :] += nn(prob.astype(jnp.bfloat16), grad)
                grad_prob = nt(rows[2, keys, :], grad)
                grad_dots = (prob * (grad_prob - correction)).astype(jnp.bfloat16)
                key_sum[keys, :] += nn(grad_dots, query)
                return query_grad_t + nn(key_t[:, keys], grad_dots)

            put(1, at, (over_keys(backward, zero) * scale).T)

        smaller = 0
        for width in WIDTHS[edge > 0]:
            pl.when((count > smaller) & (count <= width))(functools.partial(tile_of, width))
            smaller = width
        if smaller < tiles:
            pl.when(count > smaller)(tile_by_steps)
        return nothing

    lax.fori_loop(0, tiles, query_tile, 0)

    def finish(t, nothing):
        at = pl.ds(pl.multiple_of(t * TILE, TILE), TILE)

        @pl.when(lo_ref[t] < hi_ref[t])
        def _():
            put(2, at, key_sum[at, :] * scale)
            put(3, at, value_sum[at, :])

        return nothing

    lax.fori_loop(0, tiles, finish, 0)
    pieces = [(result_ref, edge)]
    if edge:
        pieces += [(to_before_ref, 0), (to_after_ref, edge + members)]
    for target, first in pieces:
        for i in range(target.shape[0]):
            for a in range(ARRAYS):
                target[i, a] = made[a, first + i]


def attend(chunk, plan, own, around=(), base=None):
    members, _, part, _ = own.shape
    edge = around[0].shape[0] if around else 0
    blocks = members + 2 * edge
    length = blocks * part
    tiles = length // TILE
    smem = pl.BlockSpec(memory_space=pltpu.SMEM)
    vmem = pl.BlockSpec(memory_space=pltpu.VMEM)
    operands = (own, *around, base) if edge else (own,)
    results = (own, *around)
    pairs = tiles * 2 * TILE * TILE
    return pl.pallas_call(
        functools.partial(attend_kernel, edge),
        in_specs=[smem, smem, vmem, vmem] + [vmem] * len(operands),
        out_specs=[vmem] * len(results),
        out_shape=[jax.ShapeDtypeStruct(x.shape, x.dtype) for x in results],
        scratch_shapes=[
            pltpu.VMEM((ARRAYS, blocks, part, DH), jnp.bfloat16),
            pltpu.VMEM((ARRAYS, blocks, part, DH), jnp.bfloat16),
            pltpu.VMEM((DH, length), jnp.bfloat16),
            pltpu.VMEM((DH, length), jnp.bfloat16),
            pltpu.VMEM((length, DH), jnp.float32),
            pltpu.VMEM((length, DH), jnp.float32),
            pltpu.VMEM((length, TILE), jnp.float32),
        ],
        compiler_params=pltpu.CompilerParams(vmem_limit_bytes=40 * 1024 * 1024),
        cost_estimate=pl.CostEstimate(
            flops=12 * pairs * DH, bytes_accessed=2 * ARRAYS * 2 * length * DH, transcendentals=pairs
        ),
        name=f"{'edge' if edge else 'inner'}{chunk}",
    )(*plan, *operands)


def merge_kernel(inside_ref, across_ref, made_ref, head_ref, tail_ref, o_ref):
    members, _, part, _ = o_ref.shape
    edge = head_ref.shape[0]
    for i in range(members):
        came = None
        if i < edge:
            came = head_ref.at[i]
        elif i >= members - edge:
            came = tail_ref.at[i - (members - edge)]
        for a in range(ARRAYS):
            new = made_ref[i, a]
            if came is not None:
                inside = inside_ref[i * part : (i + 1) * part, :]
                across = across_ref[(edge + i) * part : (edge + i + 1) * part, :]
                mine = jnp.maximum(inside, across) >= 0
                new = jnp.where(mine, new.astype(jnp.float32), came[a].astype(jnp.float32))
            o_ref[i, a] = new.astype(jnp.bfloat16)


def merge(chunk, inside, across, made, head, tail):
    vmem = pl.BlockSpec(memory_space=pltpu.VMEM)
    return pl.pallas_call(
        merge_kernel,
        in_specs=[vmem] * 5,
        out_specs=vmem,
        out_shape=jax.ShapeDtypeStruct(made.shape, jnp.bfloat16),
        compiler_params=pltpu.CompilerParams(vmem_limit_bytes=16 * 1024 * 1024),
        cost_estimate=pl.CostEstimate(flops=0, bytes_accessed=6 * made.size, transcendentals=0),
        name=f"merge{chunk}",
    )(inside[-1], across[-1], made, head, tail)


def clip_plans(clip_lengths, shard, own_rows, edge_rows):
    count = clip_lengths.shape[0]
    order = jnp.arange(count, dtype=jnp.int32)
    upto = order[:, None] >= order[None, :]
    ends = jnp.sum(jnp.where(upto, clip_lengths[None, :], 0), axis=1)
    starts = ends - clip_lengths
    first, last = starts // own_rows, (ends - 1) // own_rows
    border = last * own_rows
    owner = jnp.where((first == last) | (ends - border > border - starts), last, first)

    def ids_of(mine, origin, length):
        positions = origin + jnp.arange(length, dtype=jnp.int32)[:, None]
        inside = mine[None, :] & (positions >= starts[None, :]) & (positions < ends[None, :])
        return jnp.sum(jnp.where(inside, order[None, :] + 1, 0), axis=1) - 1

    def plan(mine, edge_rows):
        length = own_rows + 2 * edge_rows
        origin = shard * own_rows - edge_rows
        ids = ids_of(mine, origin, length)
        tiles = length // TILE
        tile_from = origin + TILE * jnp.arange(tiles, dtype=jnp.int32)[:, None]
        meets = mine[None, :] & (starts[None, :] < tile_from + TILE) & (ends[None, :] > tile_from)
        low = jnp.min(jnp.where(meets, starts[None, :] - origin, length), axis=1) // TILE
        high = (jnp.max(jnp.where(meets, ends[None, :] - origin, 0), axis=1) + TILE - 1) // TILE
        return low, high, ids.reshape(tiles, TILE), jnp.broadcast_to(ids[:, None], (length, DH))

    mine = owner == shard
    return plan(mine & (first == last), 0), plan(mine & (first != last), edge_rows)


def per_device(query_rows, key_rows, value_rows, out_grad, clip_lengths):
    part, features = query_rows.shape
    members = lax.axis_size(GROUP)
    chunks = features // (members * DH)
    shards = lax.axis_size(CHAIN)
    shard = lax.axis_index(CHAIN)
    own_rows = members * part
    edge = LONGEST // 2 // part
    inside, across = clip_plans(clip_lengths, shard, own_rows, edge * part)
    upward = [(i, i + 1) for i in range(shards - 1)]
    downward = [(i + 1, i) for i in range(shards - 1)]

    arrays = (query_rows, key_rows, value_rows, out_grad)
    tie = lax.optimization_barrier
    swap = functools.partial(lax.all_to_all, axis_name=GROUP, split_axis=0, concat_axis=0, tiled=True)

    def around(own):
        return (
            lax.ppermute(own[members - edge :], CHAIN, upward),
            lax.ppermute(own[:edge], CHAIN, downward),
        )

    def back(parts):
        made, to_before, to_after = parts
        head = lax.ppermute(to_after, CHAIN, upward)
        return made, head, lax.ppermute(to_before, CHAIN, downward)

    def compute(chunk, own):
        [base] = attend(chunk, inside, own)
        return attend(chunk, across, own, around(own), base)

    packed = [pack(chunk, members, arrays) for chunk in range(chunks)]
    last = chunks - 1
    own, made, sent, ready, got = {}, {}, {}, {}, {}
    own[0] = swap(packed[0])
    own[0], packed[1:] = tie((own[0], packed[1:]))
    for chunk in range(1, chunks):
        if chunk >= 2:
            packed[chunk], own[chunk - 1], made[chunk - 2] = tie(
                (packed[chunk], own[chunk - 1], made[chunk - 2])
            )
            sent[chunk - 2] = back(made[chunk - 2])
        else:
            packed[chunk], own[chunk - 1] = tie((packed[chunk], own[chunk - 1]))
        own[chunk] = swap(packed[chunk])
        made[chunk - 1] = compute(chunk - 1, own[chunk - 1])
    results = ()
    for chunk in range(chunks):
        if chunk < last:
            late = last - 1 + chunk
            sent[chunk], made[late] = tie((sent[chunk], made[late]))
        ready[chunk] = merge(chunk, inside, across, *sent[chunk])
        if chunk == 0:
            ready[0], own[last], made[last - 1] = tie((ready[0], own[last], made[last - 1]))
            sent[last - 1] = back(made[last - 1])
            made[last] = compute(last, own[last])
        elif chunk == 1:
            ready[1], got[0], made[last] = tie((ready[1], got[0], made[last]))
            sent[last] = back(made[last])
        else:
            ready[chunk], got[chunk - 1] = tie((ready[chunk], got[chunk - 1]))
        got[chunk] = swap(ready[chunk])
        if chunk:
            results = unpack(chunk - 1, chunks, got[chunk - 1], results)
    return tuple(unpack(last, chunks, got[last], results))


def solution(mesh):
    enc, ctx, tp = mesh.devices.shape
    fine = Mesh(mesh.devices.reshape(enc, ctx // 2, 2, tp), ("yl", "z", "yh", "tp"))
    rows = P(("yl", "z", "yh", "tp"), None)
    return jax.shard_map(
        per_device,
        mesh=fine,
        in_specs=(rows,) * ARRAYS + (P(),),
        out_specs=(rows,) * ARRAYS,
        check_vma=False,
    )
```

```python
import functools

import jax
import jax.numpy as jnp
from jax import lax
from jax.experimental import pallas as pl
from jax.experimental.pallas import tpu as pltpu
from jax.sharding import Mesh, PartitionSpec as P

DH = 128
ARRAYS = 4
TILE = 256
WIDTHS = {False: (2, 3, 4, 6), True: (2, 3, 4)}
GROUP = ("yh", "tp")
CHAIN = ("yl", "z")
LONGEST = 768
LOG2E = 1.4426950408889634
MASKED = -1e30


def pack_kernel(q_ref, k_ref, v_ref, g_ref, o_ref):
    for j in range(o_ref.shape[0]):
        for a, ref in enumerate((q_ref, k_ref, v_ref, g_ref)):
            o_ref[j, a] = ref[:, j * DH : (j + 1) * DH]


def pack(chunk, members, arrays):
    rows = arrays[0].shape[0]
    step = members
    steps = members // step
    spec = pl.BlockSpec((rows, step * DH), lambda i: (0, chunk * steps + i))
    size = members * ARRAYS * rows * DH
    return pl.pallas_call(
        pack_kernel,
        grid=(steps,),
        in_specs=[spec] * ARRAYS,
        out_specs=pl.BlockSpec((step, ARRAYS, rows, DH), lambda i: (i, 0, 0, 0)),
        out_shape=jax.ShapeDtypeStruct((members, ARRAYS, rows, DH), jnp.bfloat16),
        cost_estimate=pl.CostEstimate(flops=0, bytes_accessed=4 * size, transcendentals=0),
        name=f"pack{chunk}",
    )(*arrays)


def unpack_kernel(r_ref, *refs):
    outs = refs[-ARRAYS:]
    for j in range(r_ref.shape[0]):
        for a, ref in enumerate(outs):
            ref[:, j * DH : (j + 1) * DH] = r_ref[j, a]


def unpack(chunk, chunks, received, earlier):
    members, _, rows, _ = received.shape
    step = members
    steps = members // step
    size = members * ARRAYS * rows * DH
    spec = pl.BlockSpec((rows, step * DH), lambda i: (0, chunk * steps + i))
    return pl.pallas_call(
        unpack_kernel,
        grid=(steps,),
        in_specs=[pl.BlockSpec(memory_space=pltpu.VMEM)]
        + [pl.BlockSpec(memory_space=pl.ANY)] * len(earlier),
        out_specs=[spec] * ARRAYS,
        out_shape=[jax.ShapeDtypeStruct((rows, chunks * members * DH), jnp.bfloat16)] * ARRAYS,
        input_output_aliases={1 + a: a for a in range(len(earlier))},
        cost_estimate=pl.CostEstimate(flops=0, bytes_accessed=4 * size, transcendentals=0),
        name=f"unpack{chunk}",
    )(received, *earlier)


def attend_kernel(edge, *refs):
    lo_ref, hi_ref, qid_ref, kid_ref, own_ref = refs[:5]
    if edge:
        before_ref, after_ref, base_ref, result_ref, to_before_ref, to_after_ref = refs[5:11]
    else:
        result_ref = refs[5]
    window, made, key_t, value_t, key_sum, value_sum, cells = refs[-7:]
    members, _, part, _ = own_ref.shape
    blocks = members + 2 * edge
    length = blocks * part
    tiles = length // TILE
    scale = DH**-0.5
    pieces = [(own_ref, edge)]
    if edge:
        pieces += [(before_ref, 0), (after_ref, edge + members)]
        for i in range(members):
            for a in range(ARRAYS):
                made[a, edge + i] = base_ref[i, a]
    for source, first in pieces:
        for i in range(source.shape[0]):
            for a in range(ARRAYS):
                window[a, first + i] = source[i, a]
    key_sum[...] = jnp.zeros_like(key_sum)
    value_sum[...] = jnp.zeros_like(value_sum)
    rows = window.reshape(ARRAYS, length, DH)
    outs = made.reshape(ARRAYS, length, DH)

    def put(a, at, new):
        if edge:
            new = jnp.where(kid_ref[at, :] >= 0, new, outs[a, at, :].astype(jnp.float32))
        outs[a, at, :] = new.astype(jnp.bfloat16)

    def turn(j, carry):
        at = pl.ds(pl.multiple_of(j * TILE, TILE), TILE)
        key_t[:, at] = rows[1, at, :].T
        value_t[:, at] = rows[2, at, :].T
        return carry

    lax.fori_loop(0, tiles, turn, 0)

    def nt(a, b):
        return lax.dot_general(a, b, (((1,), (1,)), ((), ())), preferred_element_type=jnp.float32)

    def nn(a, b):
        return jnp.dot(a, b, preferred_element_type=jnp.float32)

    def query_tile(t, nothing):
        at = pl.ds(pl.multiple_of(t * TILE, TILE), TILE)
        low, count = lo_ref[t], hi_ref[t] - lo_ref[t]

        def tile_of(width):
            size = width * TILE
            first = jnp.minimum(low, tiles - width) * TILE
            keys = pl.ds(pl.multiple_of(first, TILE), size)
            query, grad = rows[0, at, :], rows[3, at, :]
            query_ids = qid_ref[pl.ds(t, 1), :]
            dots = nt(rows[1, keys, :], query)
            ids = kid_ref[keys, :]
            ids = jnp.concatenate([ids] * (TILE // DH), axis=1)
            dots = jnp.where(ids == query_ids, dots, MASKED)
            top = jnp.max(dots, axis=0, keepdims=True)
            weights = jnp.exp2((dots - top) * (scale * LOG2E))
            total = jnp.sum(weights, axis=0, keepdims=True)
            half = weights.astype(jnp.bfloat16)
            inverse = jnp.where(query_ids >= 0, 1.0 / total, 0.0)
            share = jnp.broadcast_to(inverse, (DH, TILE)).T
            out_t = nn(value_t[:, keys], half) * inverse
            grad_prob = nt(rows[2, keys, :], grad)
            correction = jnp.sum(grad.astype(jnp.float32).T * out_t, axis=0, keepdims=True)
            put(0, at, out_t.T)
            value_sum[keys, :] += nn(half, (grad.astype(jnp.float32) * share).astype(jnp.bfloat16))
            grad_dots = (weights * (grad_prob - correction)).astype(jnp.bfloat16)
            key_sum[keys, :] += nn(
                grad_dots, (query.astype(jnp.float32) * share).astype(jnp.bfloat16)
            )
            put(1, at, (nn(key_t[:, keys], grad_dots) * (inverse * scale)).T)

        def tile_by_steps():
            query, grad = rows[0, at, :], rows[3, at, :]
            query_ids = qid_ref[pl.ds(t, 1), :]

            def over_keys(body, carry):
                def step(j, carry):
                    return body(pl.ds(pl.multiple_of(j * TILE, TILE), TILE), carry)

                return lax.fori_loop(low, low + count, step, carry)

            def scores(keys, top):
                dots = nt(rows[1, keys, :], query)
                ids = kid_ref[keys, :]
                ids = jnp.concatenate([ids] * (TILE // DH), axis=1)
                dots = jnp.where(ids == query_ids, dots, MASKED)
                cells[keys, :] = dots
                return jnp.maximum(top, jnp.max(dots, axis=0, keepdims=True))

            top = over_keys(scores, jnp.full((1, TILE), MASKED, jnp.float32))

            def weigh(keys, sums):
                total, out_t = sums
                weights = jnp.exp2((cells[keys, :] - top) * (scale * LOG2E))
                cells[keys, :] = weights
                total = total + jnp.sum(weights, axis=0, keepdims=True)
                return total, out_t + nn(value_t[:, keys], weights.astype(jnp.bfloat16))

            zero = jnp.zeros((DH, TILE), jnp.float32)
            total, out_t = over_keys(weigh, (jnp.zeros((1, TILE), jnp.float32), zero))
            inverse = jnp.where(query_ids >= 0, 1.0 / total, 0.0)
            out_t = out_t * inverse
            correction = jnp.sum(grad.astype(jnp.float32).T * out_t, axis=0, keepdims=True)
            put(0, at, out_t.T)

            def backward(keys, query_grad_t):
                prob = cells[keys, :] * inverse
                value_sum[keys, :] += nn(prob.astype(jnp.bfloat16), grad)
                grad_prob = nt(rows[2, keys, :], grad)
                grad_dots = (prob * (grad_prob - correction)).astype(jnp.bfloat16)
                key_sum[keys, :] += nn(grad_dots, query)
                return query_grad_t + nn(key_t[:, keys], grad_dots)

            put(1, at, (over_keys(backward, zero) * scale).T)

        smaller = 0
        for width in WIDTHS[edge > 0]:
            pl.when((count > smaller) & (count <= width))(functools.partial(tile_of, width))
            smaller = width
        if smaller < tiles:
            pl.when(count > smaller)(tile_by_steps)
        return nothing

    lax.fori_loop(0, tiles, query_tile, 0)

    def finish(t, nothing):
        at = pl.ds(pl.multiple_of(t * TILE, TILE), TILE)

        @pl.when(lo_ref[t] < hi_ref[t])
        def _():
            put(2, at, key_sum[at, :] * scale)
            put(3, at, value_sum[at, :])

        return nothing

    lax.fori_loop(0, tiles, finish, 0)
    pieces = [(result_ref, edge)]
    if edge:
        pieces += [(to_before_ref, 0), (to_after_ref, edge + members)]
    for target, first in pieces:
        for i in range(target.shape[0]):
            for a in range(ARRAYS):
                target[i, a] = made[a, first + i]


def attend(chunk, plan, own, around=(), base=None):
    members, _, part, _ = own.shape
    edge = around[0].shape[0] if around else 0
    blocks = members + 2 * edge
    length = blocks * part
    tiles = length // TILE
    smem = pl.BlockSpec(memory_space=pltpu.SMEM)
    vmem = pl.BlockSpec(memory_space=pltpu.VMEM)
    operands = (own, *around, base) if edge else (own,)
    results = (own, *around)
    pairs = tiles * 2 * TILE * TILE
    return pl.pallas_call(
        functools.partial(attend_kernel, edge),
        in_specs=[smem, smem, vmem, vmem] + [vmem] * len(operands),
        out_specs=[vmem] * len(results),
        out_shape=[jax.ShapeDtypeStruct(x.shape, x.dtype) for x in results],
        scratch_shapes=[
            pltpu.VMEM((ARRAYS, blocks, part, DH), jnp.bfloat16),
            pltpu.VMEM((ARRAYS, blocks, part, DH), jnp.bfloat16),
            pltpu.VMEM((DH, length), jnp.bfloat16),
            pltpu.VMEM((DH, length), jnp.bfloat16),
            pltpu.VMEM((length, DH), jnp.float32),
            pltpu.VMEM((length, DH), jnp.float32),
            pltpu.VMEM((length, TILE), jnp.float32),
        ],
        compiler_params=pltpu.CompilerParams(vmem_limit_bytes=40 * 1024 * 1024),
        cost_estimate=pl.CostEstimate(
            flops=12 * pairs * DH, bytes_accessed=2 * ARRAYS * 2 * length * DH, transcendentals=pairs
        ),
        name=f"{'edge' if edge else 'inner'}{chunk}",
    )(*plan, *operands)


def merge_kernel(inside_ref, across_ref, made_ref, head_ref, tail_ref, o_ref):
    members, _, part, _ = o_ref.shape
    edge = head_ref.shape[0]
    for i in range(members):
        came = None
        if i < edge:
            came = head_ref.at[i]
        elif i >= members - edge:
            came = tail_ref.at[i - (members - edge)]
        for a in range(ARRAYS):
            new = made_ref[i, a]
            if came is not None:
                inside = inside_ref[i * part : (i + 1) * part, :]
                across = across_ref[(edge + i) * part : (edge + i + 1) * part, :]
                mine = jnp.maximum(inside, across) >= 0
                new = jnp.where(mine, new.astype(jnp.float32), came[a].astype(jnp.float32))
            o_ref[i, a] = new.astype(jnp.bfloat16)


def merge(chunk, inside, across, made, head, tail):
    vmem = pl.BlockSpec(memory_space=pltpu.VMEM)
    return pl.pallas_call(
        merge_kernel,
        in_specs=[vmem] * 5,
        out_specs=vmem,
        out_shape=jax.ShapeDtypeStruct(made.shape, jnp.bfloat16),
        compiler_params=pltpu.CompilerParams(vmem_limit_bytes=16 * 1024 * 1024),
        cost_estimate=pl.CostEstimate(flops=0, bytes_accessed=6 * made.size, transcendentals=0),
        name=f"merge{chunk}",
    )(inside[-1], across[-1], made, head, tail)


def clip_plans(clip_lengths, shard, own_rows, edge_rows):
    count = clip_lengths.shape[0]
    order = jnp.arange(count, dtype=jnp.int32)
    upto = order[:, None] >= order[None, :]
    ends = jnp.sum(jnp.where(upto, clip_lengths[None, :], 0), axis=1)
    starts = ends - clip_lengths
    first, last = starts // own_rows, (ends - 1) // own_rows
    border = last * own_rows
    owner = jnp.where((first == last) | (ends - border > border - starts), last, first)

    def ids_of(mine, origin, length):
        positions = origin + jnp.arange(length, dtype=jnp.int32)[:, None]
        inside = mine[None, :] & (positions >= starts[None, :]) & (positions < ends[None, :])
        return jnp.sum(jnp.where(inside, order[None, :] + 1, 0), axis=1) - 1

    def plan(mine, edge_rows):
        length = own_rows + 2 * edge_rows
        origin = shard * own_rows - edge_rows
        ids = ids_of(mine, origin, length)
        tiles = length // TILE
        tile_from = origin + TILE * jnp.arange(tiles, dtype=jnp.int32)[:, None]
        meets = mine[None, :] & (starts[None, :] < tile_from + TILE) & (ends[None, :] > tile_from)
        low = jnp.min(jnp.where(meets, starts[None, :] - origin, length), axis=1) // TILE
        high = (jnp.max(jnp.where(meets, ends[None, :] - origin, 0), axis=1) + TILE - 1) // TILE
        return low, high, ids.reshape(tiles, TILE), jnp.broadcast_to(ids[:, None], (length, DH))

    mine = owner == shard
    return plan(mine & (first == last), 0), plan(mine & (first != last), edge_rows)


def per_device(query_rows, key_rows, value_rows, out_grad, clip_lengths):
    part, features = query_rows.shape
    members = lax.axis_size(GROUP)
    chunks = features // (members * DH)
    shards = lax.axis_size(CHAIN)
    shard = lax.axis_index(CHAIN)
    own_rows = members * part
    edge = LONGEST // 2 // part
    inside, across = clip_plans(clip_lengths, shard, own_rows, edge * part)
    upward = [(i, i + 1) for i in range(shards - 1)]
    downward = [(i + 1, i) for i in range(shards - 1)]

    arrays = (query_rows, key_rows, value_rows, out_grad)
    tie = lax.optimization_barrier
    swap = functools.partial(lax.all_to_all, axis_name=GROUP, split_axis=0, concat_axis=0, tiled=True)

    def around(own):
        return (
            lax.ppermute(own[members - edge :], CHAIN, upward),
            lax.ppermute(own[:edge], CHAIN, downward),
        )

    def back(parts):
        made, to_before, to_after = parts
        head = lax.ppermute(to_after, CHAIN, upward)
        return made, head, lax.ppermute(to_before, CHAIN, downward)

    def compute(chunk, own):
        [base] = attend(chunk, inside, own)
        return attend(chunk, across, own, around(own), base)

    packed = [pack(chunk, members, arrays) for chunk in range(chunks)]
    last = chunks - 1
    own, halo, base, sent, ready, got = {}, {}, {}, {}, {}, {}
    own[0] = swap(packed[0])
    own[0], packed[1:] = tie((own[0], packed[1:]))
    results = ()
    for chunk in range(chunks):
        turn = own[chunk]
        if chunk < last:
            packed[chunk + 1], turn = tie((packed[chunk + 1], turn))
        if chunk:
            base[chunk - 1], turn = tie((base[chunk - 1], turn))
        if chunk == 1:
            packed[2:], base[0], halo[0] = tie((packed[2:], base[0], halo[0]))
        if chunk < last:
            own[chunk + 1] = swap(packed[chunk + 1])
        else:
            ready[chunk - 2], turn, halo[chunk - 1] = tie((ready[chunk - 2], turn, halo[chunk - 1]))
            got[0] = swap(ready[0])
        own[chunk] = turn
        halo[chunk] = around(turn)
        if chunk:
            made = attend(chunk - 1, across, own[chunk - 1], halo[chunk - 1], base[chunk - 1])
            made, turn = tie((made, turn))
            sent[chunk - 1] = back(made)
        [base[chunk]] = attend(chunk, inside, turn)
        if chunk:
            sent[chunk - 1], base[chunk] = tie((sent[chunk - 1], base[chunk]))
            ready[chunk - 1] = merge(chunk - 1, inside, across, *sent[chunk - 1])
    ready[last - 1], got[0], base[last], halo[last] = tie(
        (ready[last - 1], got[0], base[last], halo[last])
    )
    got[1] = swap(ready[last - 1])
    sent[last] = back(attend(last, across, own[last], halo[last], base[last]))
    ready[last] = merge(last, inside, across, *sent[last])
    ready[last], got[1] = tie((ready[last], got[1]))
    got[last] = swap(ready[last])
    for chunk in range(chunks):
        results = unpack(chunk, chunks, got[chunk], results)
    return tuple(results)


def solution(mesh):
    enc, ctx, tp = mesh.devices.shape
    fine = Mesh(mesh.devices.reshape(enc, ctx // 2, 2, tp), ("yl", "z", "yh", "tp"))
    rows = P(("yl", "z", "yh", "tp"), None)
    return jax.shard_map(
        per_device,
        mesh=fine,
        in_specs=(rows,) * ARRAYS + (P(),),
        out_specs=(rows,) * ARRAYS,
        check_vma=False,
    )
```

```python
import functools

import jax
import jax.numpy as jnp
from jax import lax
from jax.experimental import pallas as pl
from jax.experimental.pallas import tpu as pltpu
from jax.sharding import Mesh, PartitionSpec as P

DH = 128
ARRAYS = 4
TILE = 256
WIDTHS = {False: (2, 3, 4, 6), True: (2, 3, 4)}
GROUP = ("yh", "tp")
CHAIN = ("yl", "z")
LONGEST = 768
LOG2E = 1.4426950408889634
MASKED = -1e30


def pack_kernel(q_ref, k_ref, v_ref, g_ref, o_ref):
    for j in range(o_ref.shape[0]):
        for a, ref in enumerate((q_ref, k_ref, v_ref, g_ref)):
            o_ref[j, a] = ref[:, j * DH : (j + 1) * DH]


def pack(chunk, members, arrays):
    rows = arrays[0].shape[0]
    step = members
    steps = members // step
    spec = pl.BlockSpec((rows, step * DH), lambda i: (0, chunk * steps + i))
    size = members * ARRAYS * rows * DH
    return pl.pallas_call(
        pack_kernel,
        grid=(steps,),
        in_specs=[spec] * ARRAYS,
        out_specs=pl.BlockSpec((step, ARRAYS, rows, DH), lambda i: (i, 0, 0, 0)),
        out_shape=jax.ShapeDtypeStruct((members, ARRAYS, rows, DH), jnp.bfloat16),
        cost_estimate=pl.CostEstimate(flops=0, bytes_accessed=4 * size, transcendentals=0),
        name=f"pack{chunk}",
    )(*arrays)


def unpack_kernel(r_ref, *refs):
    outs = refs[-ARRAYS:]
    for j in range(r_ref.shape[0]):
        for a, ref in enumerate(outs):
            ref[:, j * DH : (j + 1) * DH] = r_ref[j, a]


def unpack(chunk, chunks, received, earlier):
    members, _, rows, _ = received.shape
    step = members
    steps = members // step
    size = members * ARRAYS * rows * DH
    spec = pl.BlockSpec((rows, step * DH), lambda i: (0, chunk * steps + i))
    return pl.pallas_call(
        unpack_kernel,
        grid=(steps,),
        in_specs=[pl.BlockSpec(memory_space=pltpu.VMEM)]
        + [pl.BlockSpec(memory_space=pl.ANY)] * len(earlier),
        out_specs=[spec] * ARRAYS,
        out_shape=[jax.ShapeDtypeStruct((rows, chunks * members * DH), jnp.bfloat16)] * ARRAYS,
        input_output_aliases={1 + a: a for a in range(len(earlier))},
        cost_estimate=pl.CostEstimate(flops=0, bytes_accessed=4 * size, transcendentals=0),
        name=f"unpack{chunk}",
    )(received, *earlier)


def attend_kernel(edge, *refs):
    lo_ref, hi_ref, qid_ref, kid_ref, own_ref = refs[:5]
    if edge:
        before_ref, after_ref, base_ref, result_ref, to_before_ref, to_after_ref = refs[5:11]
    else:
        result_ref = refs[5]
    window, made, key_t, value_t, key_sum, value_sum, cells = refs[-7:]
    members, _, part, _ = own_ref.shape
    blocks = members + 2 * edge
    length = blocks * part
    tiles = length // TILE
    scale = DH**-0.5
    pieces = [(own_ref, edge)]
    if edge:
        pieces += [(before_ref, 0), (after_ref, edge + members)]
        for i in range(members):
            for a in range(ARRAYS):
                made[a, edge + i] = base_ref[i, a]
    for source, first in pieces:
        for i in range(source.shape[0]):
            for a in range(ARRAYS):
                window[a, first + i] = source[i, a]
    key_sum[...] = jnp.zeros_like(key_sum)
    value_sum[...] = jnp.zeros_like(value_sum)
    rows = window.reshape(ARRAYS, length, DH)
    outs = made.reshape(ARRAYS, length, DH)

    def put(a, at, new):
        if edge:
            new = jnp.where(kid_ref[at, :] >= 0, new, outs[a, at, :].astype(jnp.float32))
        outs[a, at, :] = new.astype(jnp.bfloat16)

    def turn(j, carry):
        at = pl.ds(pl.multiple_of(j * TILE, TILE), TILE)
        key_t[:, at] = rows[1, at, :].T
        value_t[:, at] = rows[2, at, :].T
        return carry

    lax.fori_loop(0, tiles, turn, 0)

    def nt(a, b):
        return lax.dot_general(a, b, (((1,), (1,)), ((), ())), preferred_element_type=jnp.float32)

    def nn(a, b):
        return jnp.dot(a, b, preferred_element_type=jnp.float32)

    def query_tile(t, nothing):
        at = pl.ds(pl.multiple_of(t * TILE, TILE), TILE)
        low, count = lo_ref[t], hi_ref[t]

        def tile_of(width):
            size = width * TILE
            first = jnp.minimum(low, length - size)
            keys = pl.ds(pl.multiple_of(first, DH), size)
            query, grad = rows[0, at, :], rows[3, at, :]
            query_ids = qid_ref[pl.ds(t, 1), :]
            dots = nt(rows[1, keys, :], query)
            ids = kid_ref[keys, :]
            ids = jnp.concatenate([ids] * (TILE // DH), axis=1)
            dots = jnp.where(ids == query_ids, dots, MASKED)
            top = jnp.max(dots, axis=0, keepdims=True)
            weights = jnp.exp2((dots - top) * (scale * LOG2E))
            total = jnp.sum(weights, axis=0, keepdims=True)
            half = weights.astype(jnp.bfloat16)
            inverse = jnp.where(query_ids >= 0, 1.0 / total, 0.0)
            share = jnp.broadcast_to(inverse, (DH, TILE)).T
            out_t = nn(value_t[:, keys], half) * inverse
            grad_prob = nt(rows[2, keys, :], grad)
            correction = jnp.sum(grad.astype(jnp.float32).T * out_t, axis=0, keepdims=True)
            put(0, at, out_t.T)
            value_sum[keys, :] += nn(half, (grad.astype(jnp.float32) * share).astype(jnp.bfloat16))
            grad_dots = (weights * (grad_prob - correction)).astype(jnp.bfloat16)
            key_sum[keys, :] += nn(
                grad_dots, (query.astype(jnp.float32) * share).astype(jnp.bfloat16)
            )
            put(1, at, (nn(key_t[:, keys], grad_dots) * (inverse * scale)).T)

        def tile_by_steps():
            query, grad = rows[0, at, :], rows[3, at, :]
            query_ids = qid_ref[pl.ds(t, 1), :]

            def over_keys(body, carry):
                def step(j, carry):
                    return body(pl.ds(pl.multiple_of(low + j * TILE, DH), TILE), carry)

                return lax.fori_loop(0, count, step, carry)

            def scores(keys, top):
                dots = nt(rows[1, keys, :], query)
                ids = kid_ref[keys, :]
                ids = jnp.concatenate([ids] * (TILE // DH), axis=1)
                dots = jnp.where(ids == query_ids, dots, MASKED)
                cells[keys, :] = dots
                return jnp.maximum(top, jnp.max(dots, axis=0, keepdims=True))

            top = over_keys(scores, jnp.full((1, TILE), MASKED, jnp.float32))

            def weigh(keys, sums):
                total, out_t = sums
                weights = jnp.exp2((cells[keys, :] - top) * (scale * LOG2E))
                cells[keys, :] = weights
                total = total + jnp.sum(weights, axis=0, keepdims=True)
                return total, out_t + nn(value_t[:, keys], weights.astype(jnp.bfloat16))

            zero = jnp.zeros((DH, TILE), jnp.float32)
            total, out_t = over_keys(weigh, (jnp.zeros((1, TILE), jnp.float32), zero))
            inverse = jnp.where(query_ids >= 0, 1.0 / total, 0.0)
            out_t = out_t * inverse
            correction = jnp.sum(grad.astype(jnp.float32).T * out_t, axis=0, keepdims=True)
            put(0, at, out_t.T)

            def backward(keys, query_grad_t):
                prob = cells[keys, :] * inverse
                value_sum[keys, :] += nn(prob.astype(jnp.bfloat16), grad)
                grad_prob = nt(rows[2, keys, :], grad)
                grad_dots = (prob * (grad_prob - correction)).astype(jnp.bfloat16)
                key_sum[keys, :] += nn(grad_dots, query)
                return query_grad_t + nn(key_t[:, keys], grad_dots)

            put(1, at, (over_keys(backward, zero) * scale).T)

        smaller = 0
        for width in WIDTHS[edge > 0]:
            pl.when((count > smaller) & (count <= width))(functools.partial(tile_of, width))
            smaller = width
        if smaller < tiles:
            pl.when(count > smaller)(tile_by_steps)
        return nothing

    lax.fori_loop(0, tiles, query_tile, 0)

    def finish(t, nothing):
        at = pl.ds(pl.multiple_of(t * TILE, TILE), TILE)

        @pl.when(hi_ref[t] > 0)
        def _():
            put(2, at, key_sum[at, :] * scale)
            put(3, at, value_sum[at, :])

        return nothing

    lax.fori_loop(0, tiles, finish, 0)
    pieces = [(result_ref, edge)]
    if edge:
        pieces += [(to_before_ref, 0), (to_after_ref, edge + members)]
    for target, first in pieces:
        for i in range(target.shape[0]):
            for a in range(ARRAYS):
                target[i, a] = made[a, first + i]


def attend(chunk, plan, own, around=(), base=None):
    members, _, part, _ = own.shape
    edge = around[0].shape[0] if around else 0
    blocks = members + 2 * edge
    length = blocks * part
    tiles = length // TILE
    smem = pl.BlockSpec(memory_space=pltpu.SMEM)
    vmem = pl.BlockSpec(memory_space=pltpu.VMEM)
    operands = (own, *around, base) if edge else (own,)
    results = (own, *around)
    pairs = tiles * 2 * TILE * TILE
    return pl.pallas_call(
        functools.partial(attend_kernel, edge),
        in_specs=[smem, smem, vmem, vmem] + [vmem] * len(operands),
        out_specs=[vmem] * len(results),
        out_shape=[jax.ShapeDtypeStruct(x.shape, x.dtype) for x in results],
        scratch_shapes=[
            pltpu.VMEM((ARRAYS, blocks, part, DH), jnp.bfloat16),
            pltpu.VMEM((ARRAYS, blocks, part, DH), jnp.bfloat16),
            pltpu.VMEM((DH, length), jnp.bfloat16),
            pltpu.VMEM((DH, length), jnp.bfloat16),
            pltpu.VMEM((length, DH), jnp.float32),
            pltpu.VMEM((length, DH), jnp.float32),
            pltpu.VMEM((length, TILE), jnp.float32),
        ],
        compiler_params=pltpu.CompilerParams(vmem_limit_bytes=40 * 1024 * 1024),
        cost_estimate=pl.CostEstimate(
            flops=12 * pairs * DH, bytes_accessed=2 * ARRAYS * 2 * length * DH, transcendentals=pairs
        ),
        name=f"{'edge' if edge else 'inner'}{chunk}",
    )(*plan, *operands)


def merge_kernel(inside_ref, across_ref, made_ref, head_ref, tail_ref, o_ref):
    members, _, part, _ = o_ref.shape
    edge = head_ref.shape[0]
    for i in range(members):
        came = None
        if i < edge:
            came = head_ref.at[i]
        elif i >= members - edge:
            came = tail_ref.at[i - (members - edge)]
        for a in range(ARRAYS):
            new = made_ref[i, a]
            if came is not None:
                inside = inside_ref[i * part : (i + 1) * part, :]
                across = across_ref[(edge + i) * part : (edge + i + 1) * part, :]
                mine = jnp.maximum(inside, across) >= 0
                new = jnp.where(mine, new.astype(jnp.float32), came[a].astype(jnp.float32))
            o_ref[i, a] = new.astype(jnp.bfloat16)


def merge(chunk, inside, across, made, head, tail):
    vmem = pl.BlockSpec(memory_space=pltpu.VMEM)
    return pl.pallas_call(
        merge_kernel,
        in_specs=[vmem] * 5,
        out_specs=vmem,
        out_shape=jax.ShapeDtypeStruct(made.shape, jnp.bfloat16),
        compiler_params=pltpu.CompilerParams(vmem_limit_bytes=16 * 1024 * 1024),
        cost_estimate=pl.CostEstimate(flops=0, bytes_accessed=6 * made.size, transcendentals=0),
        name=f"merge{chunk}",
    )(inside[-1], across[-1], made, head, tail)


def clip_plans(clip_lengths, shard, own_rows, edge_rows):
    count = clip_lengths.shape[0]
    order = jnp.arange(count, dtype=jnp.int32)
    upto = order[:, None] >= order[None, :]
    ends = jnp.sum(jnp.where(upto, clip_lengths[None, :], 0), axis=1)
    starts = ends - clip_lengths
    first, last = starts // own_rows, (ends - 1) // own_rows
    border = last * own_rows
    owner = jnp.where((first == last) | (ends - border > border - starts), last, first)

    def ids_of(mine, origin, length):
        positions = origin + jnp.arange(length, dtype=jnp.int32)[:, None]
        inside = mine[None, :] & (positions >= starts[None, :]) & (positions < ends[None, :])
        return jnp.sum(jnp.where(inside, order[None, :] + 1, 0), axis=1) - 1

    def plan(mine, edge_rows):
        length = own_rows + 2 * edge_rows
        origin = shard * own_rows - edge_rows
        ids = ids_of(mine, origin, length)
        tiles = length // TILE
        tile_from = origin + TILE * jnp.arange(tiles, dtype=jnp.int32)[:, None]
        meets = mine[None, :] & (starts[None, :] < tile_from + TILE) & (ends[None, :] > tile_from)
        low = jnp.min(jnp.where(meets, starts[None, :] - origin, length), axis=1) // DH * DH
        high = jnp.max(jnp.where(meets, ends[None, :] - origin, 0), axis=1)
        steps = jnp.maximum(high - low + TILE - 1, 0) // TILE
        low = jnp.minimum(low, length - steps * TILE)
        return low, steps, ids.reshape(tiles, TILE), jnp.broadcast_to(ids[:, None], (length, DH))

    mine = owner == shard
    return plan(mine & (first == last), 0), plan(mine & (first != last), edge_rows)


def per_device(query_rows, key_rows, value_rows, out_grad, clip_lengths):
    part, features = query_rows.shape
    members = lax.axis_size(GROUP)
    chunks = features // (members * DH)
    shards = lax.axis_size(CHAIN)
    shard = lax.axis_index(CHAIN)
    own_rows = members * part
    edge = LONGEST // 2 // part
    inside, across = clip_plans(clip_lengths, shard, own_rows, edge * part)
    upward = [(i, i + 1) for i in range(shards - 1)]
    downward = [(i + 1, i) for i in range(shards - 1)]

    arrays = (query_rows, key_rows, value_rows, out_grad)
    tie = lax.optimization_barrier
    swap = functools.partial(lax.all_to_all, axis_name=GROUP, split_axis=0, concat_axis=0, tiled=True)

    def around(own):
        return (
            lax.ppermute(own[members - edge :], CHAIN, upward),
            lax.ppermute(own[:edge], CHAIN, downward),
        )

    def back(parts):
        made, to_before, to_after = parts
        head = lax.ppermute(to_after, CHAIN, upward)
        return made, head, lax.ppermute(to_before, CHAIN, downward)

    def compute(chunk, own):
        [base] = attend(chunk, inside, own)
        return attend(chunk, across, own, around(own), base)

    packed = [pack(chunk, members, arrays) for chunk in range(chunks)]
    last = chunks - 1
    own, halo, base, sent, ready, got = {}, {}, {}, {}, {}, {}
    own[0] = swap(packed[0])
    own[0], packed[1:] = tie((own[0], packed[1:]))
    results = ()
    for chunk in range(chunks):
        turn = own[chunk]
        if chunk < last:
            packed[chunk + 1], turn = tie((packed[chunk + 1], turn))
        if chunk:
            base[chunk - 1], turn = tie((base[chunk - 1], turn))
        if chunk == 1:
            packed[2:], base[0], halo[0] = tie((packed[2:], base[0], halo[0]))
        if chunk < last:
            own[chunk + 1] = swap(packed[chunk + 1])
        else:
            ready[chunk - 2], turn, halo[chunk - 1] = tie((ready[chunk - 2], turn, halo[chunk - 1]))
            got[0] = swap(ready[0])
        own[chunk] = turn
        halo[chunk] = around(turn)
        if chunk:
            made = attend(chunk - 1, across, own[chunk - 1], halo[chunk - 1], base[chunk - 1])
            made, turn = tie((made, turn))
            sent[chunk - 1] = back(made)
        [base[chunk]] = attend(chunk, inside, turn)
        if chunk:
            sent[chunk - 1], base[chunk] = tie((sent[chunk - 1], base[chunk]))
            ready[chunk - 1] = merge(chunk - 1, inside, across, *sent[chunk - 1])
    ready[last - 1], got[0], base[last], halo[last] = tie(
        (ready[last - 1], got[0], base[last], halo[last])
    )
    got[1] = swap(ready[last - 1])
    sent[last] = back(attend(last, across, own[last], halo[last], base[last]))
    ready[last] = merge(last, inside, across, *sent[last])
    ready[last], got[1] = tie((ready[last], got[1]))
    got[last] = swap(ready[last])
    for chunk in range(chunks):
        results = unpack(chunk, chunks, got[chunk], results)
    return tuple(results)


def solution(mesh):
    enc, ctx, tp = mesh.devices.shape
    fine = Mesh(mesh.devices.reshape(enc, ctx // 2, 2, tp), ("yl", "z", "yh", "tp"))
    rows = P(("yl", "z", "yh", "tp"), None)
    return jax.shard_map(
        per_device,
        mesh=fine,
        in_specs=(rows,) * ARRAYS + (P(),),
        out_specs=(rows,) * ARRAYS,
        check_vma=False,
    )
```
